128 devices in a mesh: tm: 16 (over z, x), chan: 8 (over y, core).
Axes of the slice: x: 4, y: 4, z: 4, core: 2. Of those that a mesh axis runs over, the one named last changes fastest.
Arguments:
- records: float32 [64, 16, 8, 16, 4096], P('tm', None, 'chan'), may hold values from -6 to 6
- band_gain: float32 [384], replicated, may hold values from 0.5 to 2
- pair_mask: int32 [128, 5], P(('tm', 'chan')), may hold values 0 or 1
Outputs:
- stacks: float32 [128, 5, 16, 16, 2, 384], P(('tm', 'chan'))
The draws below stay inside these ranges and needn't reach their ends.
All inputs are finite; a program needn't handle non-finite values. No bound on the sum of `pair_mask` on one device may be relied on, other than what follows from the above.
Results may differ from the reference program's by a relative error of at most 0.0031.
Values may be sent and summed in bfloat16 or wider, within the bound.
A program may use at most 256 MiB of HBM per device.

```python
import math
import jax
import jax.numpy as jnp
from jax import lax

L = 4096
F0 = 8
HW = 64
NB = 384
REACH = 4
BS = 16
WIN = 64
TMB = 16
CHB = 8
NBLK = 128
N_TM = 16
N_CHAN = 8


def touch_ends(values, rng, smallest, high):
    spot = [jax.random.randint(jax.random.fold_in(rng, axis), (), 0, length) for axis, length in enumerate(values.shape)]
    longest = values.shape.index(max(values.shape))
    next_to = spot[:longest] + [(spot[longest] + 1) % values.shape[longest]] + spot[longest + 1:]
    return values.at[tuple(spot)].set(smallest).at[tuple(next_to)].set(high)


def levels(key, shape, pieces, low, high):
    def one(dim, parts):
        steps = jax.random.uniform(jax.random.fold_in(jax.random.fold_in(key, 6), dim), (parts,), jnp.float32, low / len(pieces), high / len(pieces))
        return jnp.repeat(jnp.exp(steps), shape[dim] // parts).reshape((-1,) + (1,) * (len(shape) - dim - 1))

    gain = one(*pieces[0])
    for cut in pieces[1:]:
        gain = gain * one(*cut)
    return gain


def scatter_about(rng, shape, spread, bound, shards=(), kind=jnp.bfloat16):
    values = spread * jax.random.normal(rng, shape, jnp.float32)
    if shards:
        values = values * levels(rng, shape, shards, -0.22, 0.18)
    return jnp.clip(values, -bound, bound).astype(kind)


def setup_inputs(seed: int = 0) -> dict:
    arg_keys = jax.random.split(jax.random.key(seed), 4)
    records = scatter_about(arg_keys[0], (WIN, TMB, CHB, BS, L), 1.0, 6.0, ((0, 16), (2, 8)), jnp.float32)
    band_gain = jnp.clip(jnp.exp(jax.random.uniform(arg_keys[1], (NB,), jnp.float32, math.log(0.5), math.log(2.0))), 0.5, 2.0)
    pair_mask = touch_ends((jax.random.randint(arg_keys[2], (NBLK, REACH + 1), 0, 4) < 3).astype(jnp.int32), jax.random.fold_in(arg_keys[2], 1), 0, 1)
    return {"records": records, "band_gain": band_gain, "pair_mask": pair_mask}


def dft_table(length, lowest, extent):
    sample = jnp.arange(length, dtype=jnp.int32)
    column = lowest + jnp.arange(extent, dtype=jnp.int32)
    phase = (sample[:, None] * column[None, :] % length).astype(jnp.float32) * (2.0 * math.pi / length)
    taper = (0.5 - 0.5 * jnp.cos(sample.astype(jnp.float32) * (2.0 * math.pi / length))) / math.sqrt(length)
    return jnp.concatenate([jnp.cos(phase) * taper[:, None], -jnp.sin(phase) * taper[:, None]], axis=1)

def whiten(rows, band_gain):
    extent = NB + 2 * HW
    table = dft_table(L, F0, extent)
    spectra = jnp.dot(rows, table, precision=lax.Precision.HIGHEST, preferred_element_type=jnp.float32)
    real_part = spectra[:, :extent]
    imag_part = spectra[:, extent:]
    power = real_part * real_part + imag_part * imag_part
    upper = jnp.arange(extent, dtype=jnp.int32)[:, None]
    lower = jnp.arange(NB, dtype=jnp.int32)[None, :]
    smoother = ((upper >= lower) & (upper <= lower + 2 * HW)).astype(jnp.float32)
    level = jnp.dot(power, smoother, precision=lax.Precision.HIGHEST, preferred_element_type=jnp.float32) / (2 * HW + 1)
    factor = band_gain[None, :] / jnp.sqrt(level + 1e-06)
    white_re = real_part[:, HW:HW + NB] * factor
    white_im = imag_part[:, HW:HW + NB] * factor
    return jnp.stack([white_re, white_im], axis=1).astype(jnp.bfloat16)

def correlate(left, right):
    left_wide = left.astype(jnp.float32)
    right_wide = right.astype(jnp.float32)
    product = jnp.einsum('wbapf,wbcqf->bacpqf', left_wide, right_wide)
    real_sum = product[:, :, :, 0, 0, :] + product[:, :, :, 1, 1, :]
    imag_sum = product[:, :, :, 1, 0, :] - product[:, :, :, 0, 1, :]
    return jnp.stack([real_sum, imag_sum], axis=3) / left.shape[0]

def reference(records, band_gain, pair_mask):
    windows = records.shape[0]
    blocks = N_TM * N_CHAN

    def one_window(record):
        rows = record.reshape(-1, L)
        return whiten(rows, band_gain).reshape(blocks, BS, 2, NB)
    spectra = lax.map(one_window, records)
    results = []
    for offset in range(REACH + 1):
        padding = jnp.zeros((windows, offset, BS, 2, NB), jnp.bfloat16)
        other = jnp.concatenate([spectra[:, offset:], padding], axis=1)
        weight = pair_mask[:, offset].astype(jnp.float32)
        results.append(correlate(spectra, other) * weight[:, None, None, None, None])
    return jnp.stack(results, axis=1)
```

```python
import jax
import jax.numpy as jnp
import ml_dtypes
import numpy as np
from jax import lax
from jax.experimental import pallas as pl
from jax.experimental.pallas import tpu as pltpu
from jax.sharding import PartitionSpec as P

L = 4096
F0 = 8
HW = 64
NB = 384
EXT = NB + 2 * HW
NTM = 16
NCHAN = 8
NBLK = NTM * NCHAN
BS = 16
WL = 4
ROWS = NTM * BS
MESH = pl.DeviceIdType.MESH
F32 = jnp.float32
BF16 = jnp.bfloat16
OWN, ABOVE, X1, X2, BELOW = range(5)


def bin_order():
    j = np.arange(EXT)
    return np.concatenate([j[j % 4 == 0], j[j % 4 == 2], j[j % 2 == 1]])


def dft_tables():
    order = bin_order()

    def parts(samples, bins):
        phase = (np.arange(samples)[:, None] * (F0 + bins)[None, :] % L) * (2 * np.pi / L)
        return np.cos(phase) / 64.0, -np.sin(phase) / 64.0

    quarter = EXT // 4
    even = []
    for r in range(2):
        even += parts(L // 4, order[r * quarter : (r + 1) * quarter])
    even = np.concatenate(even, axis=1)
    odd = np.concatenate(parts(L // 2, order[2 * quarter :]), axis=1)

    def split(table):
        high = table.astype(ml_dtypes.bfloat16)
        low = (table - high.astype(np.float64)).astype(ml_dtypes.bfloat16)
        return np.stack([high, low])

    return np.concatenate([split(even), split(odd)], axis=1)


def smoother_table():
    order = bin_order()
    lower = order - HW
    covered = (order[:, None] >= lower[None, :]) & (order[:, None] <= lower[None, :] + 2 * HW)
    return covered.astype(ml_dtypes.bfloat16)


def order_table():
    order = bin_order()
    return (order[:, None] == np.arange(NB)[None, :] + HW).astype(ml_dtypes.bfloat16)


def hann_row():
    n = np.arange(L)
    return (0.5 - 0.5 * np.cos(2 * np.pi * n / L)).astype(np.float32)[None, :]


def device_of(block):
    wrapped = lax.rem(block + NBLK, NBLK)
    return (wrapped // NCHAN, lax.rem(wrapped, NCHAN))


def kernel(
    rec,
    tab_hbm,
    smooth,
    perm,
    hann,
    gain,
    mask,
    out,
    xbuf,
    tab,
    fold,
    spec,
    pw,
    lev,
    wh,
    gperm,
    send,
    blocks,
    wide,
    acc,
    give,
    take,
    rec_sem,
    tab_sem,
    a2a_s,
    a2a_r,
    ring_s,
    ring_r,
    sib_s,
    sib_r,
    give_s,
    give_r,
    out_sem,
):
    t = lax.axis_index("tm")
    c = lax.axis_index("chan")
    block = t * NCHAN + c
    core = lax.rem(c, 2)
    before = device_of(block - 2)
    after = device_of(block + 2)
    sibling = (t, c + 1 - 2 * core)

    def rec_copy(w):
        slot = lax.rem(w, 2)
        return pltpu.make_async_copy(rec.at[w], xbuf.at[slot], rec_sem.at[slot])

    tab_copy = pltpu.make_async_copy(tab_hbm, tab, tab_sem)
    rec_copy(0).start()
    tab_copy.start()
    rec_copy(1).start()

    barrier = pltpu.get_barrier_semaphore()
    for d in range(1, NTM):
        pl.semaphore_signal(
            barrier, inc=1, device_id=(lax.rem(t + d, NTM), c), device_id_type=MESH
        )
    for peer in (before, after, sibling):
        pl.semaphore_signal(barrier, inc=1, device_id=peer, device_id_type=MESH)

    def clear(i, _):
        acc[i // 16, lax.rem(i, 16)] = jnp.zeros((2, BS, NB), F32)
        return 0

    lax.fori_loop(0, 80, clear, 0)

    rest = jnp.broadcast_to(gain[...], (16, NB))
    total = jnp.zeros((16, EXT), F32)
    for _ in range(3):
        piece = rest.astype(BF16)
        rest = rest - piece.astype(F32)
        total += lax.dot_general(
            piece, perm[...], (((1,), (1,)), ((), ())), preferred_element_type=F32
        )
    gperm[...] = total

    def a2a_copy(w, d):
        q = lax.rem(t + d, NTM)
        return pltpu.make_async_remote_copy(
            src_ref=send.at[w, pl.ds(pl.multiple_of(q * BS, BS), BS)],
            dst_ref=blocks.at[OWN, w, t],
            send_sem=a2a_s.at[w, d],
            recv_sem=a2a_r.at[w, d],
            device_id=(q, c),
            device_id_type=MESH,
        )

    def ring_copy(w, up):
        return pltpu.make_async_remote_copy(
            src_ref=blocks.at[OWN, w],
            dst_ref=blocks.at[ABOVE if up else BELOW, w],
            send_sem=ring_s.at[w, up],
            recv_sem=ring_r.at[w, up],
            device_id=before if up else after,
            device_id_type=MESH,
        )

    def sib_copy(w, source, slot):
        return pltpu.make_async_remote_copy(
            src_ref=blocks.at[source, w],
            dst_ref=blocks.at[slot, w],
            send_sem=sib_s.at[w, slot - X1],
            recv_sem=sib_r.at[w, slot - X1],
            device_id=sibling,
            device_id_type=MESH,
        )

    def widen(which, source, w):
        def one(i, _):
            wide[which, w, i] = blocks[source, w, i].astype(F32)
            return 0

        lax.fori_loop(0, NTM, one, 0)

    def spread(w):
        for d in range(1, NTM):
            a2a_copy(w, d).wait_recv()
        ring_copy(w, 1).start()
        ring_copy(w, 0).start()

        @pl.when(core == 1)
        def _():
            sib_copy(w, OWN, X1).start()

        widen(0, OWN, w)

    def transform(w, _):
        slot = lax.rem(w, 2)
        rec_copy(w).wait()

        def fold_rows(i, _):
            rows = pl.ds(pl.multiple_of(i * 16, 16), 16)
            low_rows = pl.ds(pl.multiple_of(ROWS + i * 16, 16), 16)

            def put(value, at):
                high = value.astype(BF16)
                fold[rows, at : at + 128] = high
                fold[low_rows, at : at + 128] = (value - high.astype(F32)).astype(BF16)

            for p in range(0, L // 4, 128):
                x0, x1, x2, x3 = (
                    xbuf[slot, rows, s + p : s + p + 128] * hann[:, s + p : s + p + 128]
                    for s in range(0, L, L // 4)
                )
                u, v = x0 + x2, x1 + x3
                put(u + v, p)
                put(u - v, L // 4 + p)
                put(x0 - x2, L // 2 + p)
                put(x1 - x3, 3 * L // 4 + p)
            return 0

        lax.fori_loop(0, ROWS // 16, fold_rows, 0)

        @pl.when(w + 2 < WL)
        def _():
            rec_copy(w + 2).start()

        @pl.when(w == 0)
        def _():
            tab_copy.wait()

        def product(at, length, trow, tcol, col):
            both = jnp.dot(
                fold[:, at : at + length],
                tab[0, trow : trow + length, tcol : tcol + 256],
                preferred_element_type=F32,
            )
            low = jnp.dot(
                fold[:ROWS, at : at + length],
                tab[1, trow : trow + length, tcol : tcol + 256],
                preferred_element_type=F32,
            )
            spec[:, col : col + 256] = both[:ROWS] + (both[ROWS:] + low)

        product(0, L // 4, 0, 0, 0)
        product(L // 4, L // 4, 0, 256, 256)
        product(L // 2, L // 2, L // 4, 0, 512)
        product(L // 2, L // 2, L // 4, 256, 768)

        def spectrum(rows):
            re = jnp.concatenate([spec[rows, 0:128], spec[rows, 256:384], spec[rows, 512:768]], 1)
            im = jnp.concatenate([spec[rows, 128:256], spec[rows, 384:512], spec[rows, 768:1024]], 1)
            return re, im

        def power_rows(i, _):
            rows = pl.ds(pl.multiple_of(i * 16, 16), 16)
            re, im = spectrum(rows)
            power = re * re + im * im
            high = power.astype(BF16)
            pw[rows] = high
            pw[pl.ds(pl.multiple_of(ROWS + i * 16, 16), 16)] = (power - high.astype(F32)).astype(BF16)
            return 0

        lax.fori_loop(0, ROWS // 16, power_rows, 0)
        lev[...] = jnp.dot(pw[...], smooth[...], preferred_element_type=F32)

        def white_rows(i, _):
            rows = pl.ds(pl.multiple_of(i * 16, 16), 16)
            low_rows = pl.ds(pl.multiple_of(ROWS + i * 16, 16), 16)
            level = (lev[rows] + lev[low_rows]) / (2 * HW + 1)
            factor = gperm[...] * lax.rsqrt(level + 1e-6)
            re, im = spectrum(rows)
            wh[rows] = (re * factor).astype(BF16)
            wh[low_rows] = (im * factor).astype(BF16)
            return 0

        lax.fori_loop(0, ROWS // 16, white_rows, 0)
        white = jnp.dot(wh[...], perm[...], preferred_element_type=F32)
        send[w, :, 0:NB] = white[:ROWS].astype(BF16)
        send[w, :, NB:] = white[ROWS:].astype(BF16)

        @pl.when(w == 0)
        def _():
            pl.semaphore_wait(barrier, NTM - 1 + 3)

        for d in range(1, NTM):
            a2a_copy(w, d).start()
        blocks[OWN, w, t] = send[w, pl.ds(pl.multiple_of(t * BS, BS), BS)]

        @pl.when(w > 0)
        def _():
            spread(w - 1)

        return 0

    lax.fori_loop(0, WL, transform, 0)

    def correlate(k, left, right, w):
        def bins(i, _):
            re_at = pl.ds(pl.multiple_of(i * 128, 128), 128)
            im_at = pl.ds(pl.multiple_of(NB + i * 128, 128), 128)
            for half in range(2):
                mine = range(half * 8, half * 8 + 8)
                start = tuple(acc[k, a, p, :, re_at] for a in mine for p in range(2))

                def window(n, sums):
                    cr = blocks[right, w, n, :, re_at].astype(F32)
                    ci = blocks[right, w, n, :, im_at].astype(F32)
                    new = []
                    for i, a in enumerate(mine):
                        ar = wide[left, w, n, a : a + 1, re_at]
                        ai = wide[left, w, n, a : a + 1, im_at]
                        new.append(sums[2 * i] + (ar * cr + ai * ci))
                        new.append(sums[2 * i + 1] + (ai * cr - ar * ci))
                    return tuple(new)

                sums = lax.fori_loop(0, NTM, window, start)
                for i, a in enumerate(mine):
                    for p in range(2):
                        acc[k, a, p, :, re_at] = sums[2 * i + p]
            return 0

        lax.fori_loop(0, NB // 128, bins, 0)

    def selfs(w, _):
        correlate(0, 0, OWN, w)
        return 0

    lax.fori_loop(0, WL - 1, selfs, 0)
    spread(WL - 1)
    correlate(0, 0, OWN, WL - 1)

    def give_copy(i):
        return pltpu.make_async_remote_copy(
            src_ref=give.at[i],
            dst_ref=take.at[i],
            send_sem=give_s.at[i],
            recv_sem=give_r.at[i],
            device_id=before,
            device_id_type=MESH,
        )

    def hand_over(i, k):
        def one(a, _):
            give[i, a] = acc[k, a].astype(BF16)
            return 0

        lax.fori_loop(0, BS, one, 0)
        give_copy(i).start()

    left3 = core
    right3 = X2 - core

    def partners(w, _):
        ring_copy(w, 1).wait_recv()

        @pl.when(core == 0)
        def _():
            sib_copy(w, ABOVE, X1).start()

        @pl.when(core == 1)
        def _():
            sib_copy(w, ABOVE, X2).start()

        ring_copy(w, 0).wait_recv()
        widen(1, BELOW, w)
        correlate(4, 1, ABOVE, w)

        @pl.when(w == WL - 1)
        def _():
            hand_over(0, 4)

        sib_copy(w, OWN, X1).wait_recv()

        @pl.when(core == 0)
        def _():
            sib_copy(w, OWN, X2).wait_recv()

        correlate(3, left3, right3, w)

        @pl.when((w == WL - 1) & (core == 1))
        def _():
            hand_over(1, 3)

        correlate(1, 0, X1, w)
        correlate(2, 0, ABOVE, w)
        return 0

    lax.fori_loop(0, WL, partners, 0)

    def out_copy(k):
        return pltpu.make_async_copy(acc.at[k], out.at[k], out_sem.at[k])

    def weight_of(k):
        inside = (block + k < NBLK).astype(F32)
        return mask[0, k].astype(F32) * inside * (1.0 / 64.0)

    def finish(k):
        weight = weight_of(k)

        def one(a, _):
            acc[k, a] = acc[k, a] * weight
            return 0

        lax.fori_loop(0, BS, one, 0)
        out_copy(k).start()

    def finish_taken(k, i):
        give_copy(i).wait_recv()
        weight = weight_of(k)

        def one(a, _):
            acc[k, a] = take[i, a].astype(F32) * weight
            return 0

        lax.fori_loop(0, BS, one, 0)
        out_copy(k).start()

    for k in range(3):
        finish(k)

    @pl.when(core == 0)
    def _():
        finish(3)

    finish_taken(4, 0)

    @pl.when(core == 1)
    def _():
        finish_taken(3, 1)

    def drain(w, _):
        for d in range(1, NTM):
            a2a_copy(w, d).wait_send()
        ring_copy(w, 1).wait_send()
        ring_copy(w, 0).wait_send()

        @pl.when(core == 0)
        def _():
            sib_copy(w, ABOVE, X1).wait_send()

        @pl.when(core == 1)
        def _():
            sib_copy(w, OWN, X1).wait_send()
            sib_copy(w, ABOVE, X2).wait_send()

        return 0

    lax.fori_loop(0, WL, drain, 0)
    give_copy(0).wait_send()

    @pl.when(core == 1)
    def _():
        give_copy(1).wait_send()

    for k in range(5):
        out_copy(k).wait()


def body(records, band_gain, pair_mask):
    rec = records.reshape(WL, ROWS, L)
    any_space = pl.BlockSpec(memory_space=pl.ANY)
    vmem = pl.BlockSpec(memory_space=pltpu.VMEM)
    smem = pl.BlockSpec(memory_space=pltpu.SMEM)
    dma = pltpu.SemaphoreType.DMA
    sums = pl.pallas_call(
        kernel,
        out_shape=jax.ShapeDtypeStruct((5, BS, 2, BS, NB), F32),
        in_specs=[any_space, any_space, vmem, vmem, vmem, vmem, smem],
        out_specs=any_space,
        scratch_shapes=[
            pltpu.VMEM((2, ROWS, L), F32),
            pltpu.VMEM((2, 3 * L // 4, 512), BF16),
            pltpu.VMEM((2 * ROWS, L), BF16),
            pltpu.VMEM((ROWS, 2 * EXT), F32),
            pltpu.VMEM((2 * ROWS, EXT), BF16),
            pltpu.VMEM((2 * ROWS, EXT), F32),
            pltpu.VMEM((2 * ROWS, EXT), BF16),
            pltpu.VMEM((16, EXT), F32),
            pltpu.VMEM((WL, ROWS, 2 * NB), BF16),
            pltpu.VMEM((5, WL, NTM, BS, 2 * NB), BF16),
            pltpu.VMEM((2, WL, NTM, BS, 2 * NB), F32),
            pltpu.VMEM((5, BS, 2, BS, NB), F32),
            pltpu.VMEM((2, BS, 2, BS, NB), BF16),
            pltpu.VMEM((2, BS, 2, BS, NB), BF16),
            dma((2,)),
            dma,
            dma((WL, NTM)),
            dma((WL, NTM)),
            dma((WL, 2)),
            dma((WL, 2)),
            dma((WL, 2)),
            dma((WL, 2)),
            dma((2,)),
            dma((2,)),
            dma((5,)),
        ],
        compiler_params=pltpu.CompilerParams(
            collective_id=0, has_side_effects=True, vmem_limit_bytes=58 << 20
        ),
        cost_estimate=pl.CostEstimate(
            flops=10**10, bytes_accessed=30 * 10**6, transcendentals=10**6
        ),
    )(
        rec,
        jnp.asarray(dft_tables()),
        jnp.asarray(smoother_table()),
        jnp.asarray(order_table()),
        jnp.asarray(hann_row()),
        band_gain[None, :],
        pair_mask,
    )
    return sums.transpose(0, 1, 3, 2, 4)[None]


def solution(mesh):
    placed = (P("tm", None, "chan", None, None), P(), P(("tm", "chan"), None))
    return jax.shard_map(
        body,
        mesh=mesh,
        in_specs=placed,
        out_specs=P(("tm", "chan"), None, None, None, None, None),
        check_vma=False,
    )
```

```python
import jax
import jax.numpy as jnp
import ml_dtypes
import numpy as np
from jax import lax
from jax.experimental import pallas as pl
from jax.experimental.pallas import tpu as pltpu
from jax.sharding import PartitionSpec as P

L = 4096
F0 = 8
HW = 64
NB = 384
EXT = NB + 2 * HW
NTM = 16
NCHAN = 8
NBLK = NTM * NCHAN
BS = 16
WL = 4
ROWS = NTM * BS
MESH = pl.DeviceIdType.MESH
F32 = jnp.float32
BF16 = jnp.bfloat16
OWN, ABOVE, X1, X2, BELOW = range(5)


def bin_order():
    j = np.arange(EXT)
    return np.concatenate([j[j % 4 == 0], j[j % 4 == 2], j[j % 2 == 1]])


def dft_tables():
    order = bin_order()

    def parts(samples, bins):
        phase = (np.arange(samples)[:, None] * (F0 + bins)[None, :] % L) * (2 * np.pi / L)
        return np.cos(phase) / 64.0, -np.sin(phase) / 64.0

    quarter = EXT // 4
    even = []
    for r in range(2):
        even += parts(L // 4, order[r * quarter : (r + 1) * quarter])
    even = np.concatenate(even, axis=1)
    odd = np.concatenate(parts(L // 2, order[2 * quarter :]), axis=1)

    def split(table):
        high = table.astype(ml_dtypes.bfloat16)
        low = (table - high.astype(np.float64)).astype(ml_dtypes.bfloat16)
        return np.stack([high, low])

    return np.concatenate([split(even), split(odd)], axis=1)


def smoother_table():
    order = bin_order()
    lower = order - HW
    covered = (order[:, None] >= lower[None, :]) & (order[:, None] <= lower[None, :] + 2 * HW)
    return covered.astype(ml_dtypes.bfloat16)


def order_table():
    order = bin_order()
    return (order[:, None] == np.arange(NB)[None, :] + HW).astype(ml_dtypes.bfloat16)


def hann_row():
    n = np.arange(L)
    return (0.5 - 0.5 * np.cos(2 * np.pi * n / L)).astype(np.float32)[None, :]


def device_of(block):
    wrapped = lax.rem(block + NBLK, NBLK)
    return (wrapped // NCHAN, lax.rem(wrapped, NCHAN))


def kernel(
    rec,
    tab_hbm,
    smooth,
    perm,
    hann,
    gain,
    mask,
    out,
    xbuf,
    tab,
    fold,
    spec,
    pw,
    lev,
    wh,
    gperm,
    send,
    blocks,
    wide,
    acc,
    give,
    take,
    rec_sem,
    tab_sem,
    a2a_s,
    a2a_r,
    dup_s,
    dup_r,
    ring_s,
    ring_r,
    sib_s,
    sib_r,
    give_s,
    give_r,
    out_sem,
):
    t = lax.axis_index("tm")
    c = lax.axis_index("chan")
    block = t * NCHAN + c
    core = lax.rem(c, 2)
    before = device_of(block - 2)
    after = device_of(block + 2)
    sibling = (t, c + 1 - 2 * core)
    first = c < 2
    last = c >= NCHAN - 2
    shift = jnp.where(first, 1, -1)
    round_corner = lax.rem(c + 6 * shift + NCHAN, NCHAN)
    dup_slot = jnp.where(first, ABOVE, BELOW)

    def rec_copy(w):
        slot = lax.rem(w, 2)
        return pltpu.make_async_copy(rec.at[w], xbuf.at[slot], rec_sem.at[slot])

    tab_copy = pltpu.make_async_copy(tab_hbm, tab, tab_sem)
    rec_copy(0).start()
    tab_copy.start()
    rec_copy(1).start()

    barrier = pltpu.get_barrier_semaphore()
    for d in range(1, NTM):
        pl.semaphore_signal(
            barrier, inc=1, device_id=(lax.rem(t + d, NTM), c), device_id_type=MESH
        )
    pl.semaphore_signal(barrier, inc=1, device_id=sibling, device_id_type=MESH)

    @pl.when(jnp.logical_not(first))
    def _():
        pl.semaphore_signal(barrier, inc=1, device_id=before, device_id_type=MESH)

    @pl.when(jnp.logical_not(last))
    def _():
        pl.semaphore_signal(barrier, inc=1, device_id=after, device_id_type=MESH)

    @pl.when(first | last)
    def _():
        for d in range(NTM):
            pl.semaphore_signal(
                barrier, inc=1, device_id=(lax.rem(t + d, NTM), round_corner), device_id_type=MESH
            )

    def clear(i, _):
        acc[i // 16, lax.rem(i, 16)] = jnp.zeros((2, BS, NB), F32)
        return 0

    lax.fori_loop(0, 80, clear, 0)

    rest = jnp.broadcast_to(gain[...].reshape(1, NB), (16, NB))
    total = jnp.zeros((16, EXT), F32)
    for _ in range(3):
        piece = rest.astype(BF16)
        rest = rest - piece.astype(F32)
        total += lax.dot_general(
            piece, perm[...], (((1,), (1,)), ((), ())), preferred_element_type=F32
        )
    gperm[...] = total

    def a2a_copy(w, d):
        q = lax.rem(t + d, NTM)
        return pltpu.make_async_remote_copy(
            src_ref=send.at[w, pl.ds(pl.multiple_of(q * BS, BS), BS)],
            dst_ref=blocks.at[OWN, w, t],
            send_sem=a2a_s.at[w, d],
            recv_sem=a2a_r.at[w, d],
            device_id=(q, c),
            device_id_type=MESH,
        )

    def dup_copy(w, d):
        r = lax.rem(t + d, NTM)
        q = lax.rem(r + shift + NTM, NTM)
        return pltpu.make_async_remote_copy(
            src_ref=send.at[w, pl.ds(pl.multiple_of(q * BS, BS), BS)],
            dst_ref=blocks.at[dup_slot, w, t],
            send_sem=dup_s.at[w, d],
            recv_sem=dup_r.at[w, d],
            device_id=(r, round_corner),
            device_id_type=MESH,
        )

    def bins_of(ref, slot, w, f):
        return ref.at[slot, w, :, :, pl.ds(pl.multiple_of(f * 256, 256), 256)]

    def ring_copy(w, up, f):
        return pltpu.make_async_remote_copy(
            src_ref=bins_of(blocks, OWN, w, f),
            dst_ref=bins_of(blocks, ABOVE if up else BELOW, w, f),
            send_sem=ring_s.at[w, f, up],
            recv_sem=ring_r.at[w, f, up],
            device_id=before if up else after,
            device_id_type=MESH,
        )

    def sib_copy(w, source, slot, f):
        return pltpu.make_async_remote_copy(
            src_ref=bins_of(blocks, source, w, f),
            dst_ref=bins_of(blocks, slot, w, f),
            send_sem=sib_s.at[w, f, slot - X1],
            recv_sem=sib_r.at[w, f, slot - X1],
            device_id=sibling,
            device_id_type=MESH,
        )

    def widen(which, source, w, f):
        at = pl.ds(pl.multiple_of(f * 256, 256), 256)

        def one(i, _):
            wide[which, w, i, :, at] = blocks[source, w, i, :, at].astype(F32)
            return 0

        lax.fori_loop(0, NTM, one, 0, unroll=4)

    def spread(w):
        for d in range(1, NTM):
            a2a_copy(w, d).wait_recv()
        for f in range(3):

            @pl.when(jnp.logical_not(first))
            def _():
                ring_copy(w, 1, f).start()

            @pl.when(jnp.logical_not(last))
            def _():
                ring_copy(w, 0, f).start()

            @pl.when(core == 1)
            def _():
                sib_copy(w, OWN, X1, f).start()

        for f in range(3):
            widen(0, OWN, w, f)

    def transform(w, _):
        slot = lax.rem(w, 2)
        rec_copy(w).wait()

        def fold_rows(i, _):
            rows = pl.ds(pl.multiple_of(i * 16, 16), 16)
            low_rows = pl.ds(pl.multiple_of(ROWS + i * 16, 16), 16)

            def put(value, at):
                high = value.astype(BF16)
                fold[rows, at : at + 128] = high
                fold[low_rows, at : at + 128] = (value - high.astype(F32)).astype(BF16)

            for p in range(0, L // 4, 128):
                x0, x1, x2, x3 = (
                    xbuf[slot, rows, s + p : s + p + 128] * hann[:, s + p : s + p + 128]
                    for s in range(0, L, L // 4)
                )
                u, v = x0 + x2, x1 + x3
                put(u + v, p)
                put(u - v, L // 4 + p)
                put(x0 - x2, L // 2 + p)
                put(x1 - x3, 3 * L // 4 + p)
            return 0

        lax.fori_loop(0, ROWS // 16, fold_rows, 0)

        @pl.when(w + 2 < WL)
        def _():
            rec_copy(w + 2).start()

        @pl.when(w == 0)
        def _():
            tab_copy.wait()

        def product(at, length, trow, tcol, col):
            both = jnp.dot(
                fold[:, at : at + length],
                tab[0, trow : trow + length, tcol : tcol + 256],
                preferred_element_type=F32,
            )
            low = jnp.dot(
                fold[:ROWS, at : at + length],
                tab[1, trow : trow + length, tcol : tcol + 256],
                preferred_element_type=F32,
            )
            spec[:, col : col + 256] = both[:ROWS] + (both[ROWS:] + low)

        product(0, L // 4, 0, 0, 0)
        product(L // 4, L // 4, 0, 256, 256)
        product(L // 2, L // 2, L // 4, 0, 512)
        product(L // 2, L // 2, L // 4, 256, 768)

        def spectrum(rows):
            re = jnp.concatenate([spec[rows, 0:128], spec[rows, 256:384], spec[rows, 512:768]], 1)
            im = jnp.concatenate([spec[rows, 128:256], spec[rows, 384:512], spec[rows, 768:1024]], 1)
            return re, im

        def power_rows(i, _):
            rows = pl.ds(pl.multiple_of(i * 16, 16), 16)
            re, im = spectrum(rows)
            power = re * re + im * im
            high = power.astype(BF16)
            pw[rows] = high
            pw[pl.ds(pl.multiple_of(ROWS + i * 16, 16), 16)] = (power - high.astype(F32)).astype(BF16)
            return 0

        lax.fori_loop(0, ROWS // 16, power_rows, 0)
        lev[...] = jnp.dot(pw[...], smooth[...], preferred_element_type=F32)

        def white_rows(i, _):
            rows = pl.ds(pl.multiple_of(i * 16, 16), 16)
            low_rows = pl.ds(pl.multiple_of(ROWS + i * 16, 16), 16)
            level = (lev[rows] + lev[low_rows]) / (2 * HW + 1)
            factor = gperm[...] * lax.rsqrt(level + 1e-6)
            re, im = spectrum(rows)
            wh[rows] = (re * factor).astype(BF16)
            wh[low_rows] = (im * factor).astype(BF16)
            return 0

        lax.fori_loop(0, ROWS // 16, white_rows, 0)
        white = jnp.dot(wh[...], perm[...], preferred_element_type=F32)
        for f in range(3):
            at = f * 256
            send[w, :, at : at + 128] = white[:ROWS, f * 128 : f * 128 + 128].astype(BF16)
            send[w, :, at + 128 : at + 256] = white[ROWS:, f * 128 : f * 128 + 128].astype(BF16)

        @pl.when((w == 0) & jnp.logical_not(first | last))
        def _():
            pl.semaphore_wait(barrier, NTM - 1 + 3)

        @pl.when((w == 0) & (first | last))
        def _():
            pl.semaphore_wait(barrier, NTM - 1 + 2 + NTM)

        for d in range(1, NTM):
            a2a_copy(w, d).start()
        blocks[OWN, w, t] = send[w, pl.ds(pl.multiple_of(t * BS, BS), BS)]

        @pl.when(w > 0)
        def _():
            spread(w - 1)

        @pl.when((w > 0) & (first | last))
        def _():
            for d in range(NTM):
                dup_copy(w - 1, d).start()

        return 0

    lax.fori_loop(0, WL, transform, 0)

    @pl.when(first | last)
    def _():
        for d in range(NTM):
            dup_copy(WL - 1, d).start()

    def correlate(k, left, right, w, f):
        re_at = pl.ds(pl.multiple_of(f * 256, 128), 128)
        im_at = pl.ds(pl.multiple_of(f * 256 + 128, 128), 128)
        at = pl.ds(pl.multiple_of(f * 128, 128), 128)
        for half in range(2):
            mine = range(half * 8, half * 8 + 8)
            start = tuple(acc[k, a, p, :, at] for a in mine for p in range(2))

            def window(n, sums):
                cr = blocks[right, w, n, :, re_at].astype(F32)
                ci = blocks[right, w, n, :, im_at].astype(F32)
                new = []
                for i, a in enumerate(mine):
                    ar = wide[left, w, n, a : a + 1, re_at]
                    ai = wide[left, w, n, a : a + 1, im_at]
                    new.append((sums[2 * i] + ar * cr) + ai * ci)
                    new.append((sums[2 * i + 1] + ai * cr) - ar * ci)
                return tuple(new)

            sums = lax.fori_loop(0, NTM, window, start, unroll=8)
            for i, a in enumerate(mine):
                for p in range(2):
                    acc[k, a, p, :, at] = sums[2 * i + p]

    def selfs(i, _):
        correlate(0, 0, OWN, i // 3, lax.rem(i, 3))
        return 0

    lax.fori_loop(0, 3 * (WL - 1), selfs, 0)
    spread(WL - 1)
    lax.fori_loop(3 * (WL - 1), 3 * WL, selfs, 0)

    def give_copy(i, f):
        return pltpu.make_async_remote_copy(
            src_ref=give.at[i, f],
            dst_ref=take.at[i, f],
            send_sem=give_s.at[i, f],
            recv_sem=give_r.at[i, f],
            device_id=before,
            device_id_type=MESH,
        )

    def hand_over(i, k, f):
        at = pl.ds(pl.multiple_of(f * 128, 128), 128)

        def one(a, _):
            give[i, f, a] = acc[k, a, :, :, at].astype(BF16)
            return 0

        lax.fori_loop(0, BS, one, 0, unroll=4)
        give_copy(i, f).start()

    left3 = core
    right3 = X2 - core

    def partners(i, _):
        w = i // 3
        f = lax.rem(i, 3)

        @pl.when(jnp.logical_not(last))
        def _():
            ring_copy(w, 1, f).wait_recv()

        @pl.when(jnp.logical_not(first))
        def _():
            ring_copy(w, 0, f).wait_recv()

        @pl.when((first | last) & (f == 0))
        def _():
            for d in range(NTM):
                dup_copy(w, d).wait_recv()

        @pl.when(core == 0)
        def _():
            sib_copy(w, ABOVE, X1, f).start()

        @pl.when(core == 1)
        def _():
            sib_copy(w, ABOVE, X2, f).start()

        widen(1, BELOW, w, f)
        correlate(4, 1, ABOVE, w, f)

        @pl.when(w == WL - 1)
        def _():
            hand_over(0, 4, f)

        correlate(2, 0, ABOVE, w, f)
        sib_copy(w, OWN, X1, f).wait_recv()

        @pl.when(core == 0)
        def _():
            sib_copy(w, OWN, X2, f).wait_recv()

        correlate(3, left3, right3, w, f)

        @pl.when((w == WL - 1) & (core == 1))
        def _():
            hand_over(1, 3, f)

        correlate(1, 0, X1, w, f)
        return 0

    def out_copy(k, p):
        return pltpu.make_async_copy(acc.at[k, :, p], out.at[k, :, :, p], out_sem.at[k, p])

    def weight_of(k):
        inside = (block + k < NBLK).astype(F32)
        return mask[0, k].astype(F32) * inside * (1.0 / 64.0)

    def finish(k):
        weight = weight_of(k)

        def one(a, _):
            acc[k, a] = acc[k, a] * weight
            return 0

        lax.fori_loop(0, BS, one, 0, unroll=2)
        for p in range(2):
            out_copy(k, p).start()

    def finish_taken(k, i):
        weight = weight_of(k)
        for f in range(3):
            give_copy(i, f).wait_recv()

            def one(a, _):
                acc[k, a, :, :, f * 128 : f * 128 + 128] = take[i, f, a].astype(F32) * weight
                return 0

            lax.fori_loop(0, BS, one, 0, unroll=4)
        for p in range(2):
            out_copy(k, p).start()

    finish(0)
    lax.fori_loop(0, 3 * WL, partners, 0)

    finish(2)
    finish(1)

    @pl.when(core == 0)
    def _():
        finish(3)

    finish_taken(4, 0)

    @pl.when(core == 1)
    def _():
        finish_taken(3, 1)

    def drain(i, _):
        w = i // 3
        f = lax.rem(i, 3)

        @pl.when(f == 0)
        def _():
            for d in range(1, NTM):
                a2a_copy(w, d).wait_send()

        @pl.when((first | last) & (f == 0))
        def _():
            for d in range(NTM):
                dup_copy(w, d).wait_send()

        @pl.when(jnp.logical_not(first))
        def _():
            ring_copy(w, 1, f).wait_send()

        @pl.when(jnp.logical_not(last))
        def _():
            ring_copy(w, 0, f).wait_send()

        @pl.when(core == 0)
        def _():
            sib_copy(w, ABOVE, X1, f).wait_send()

        @pl.when(core == 1)
        def _():
            sib_copy(w, OWN, X1, f).wait_send()
            sib_copy(w, ABOVE, X2, f).wait_send()

        return 0

    lax.fori_loop(0, 3 * WL, drain, 0)
    for f in range(3):
        give_copy(0, f).wait_send()

        @pl.when(core == 1)
        def _():
            give_copy(1, f).wait_send()

    for k in range(5):
        for p in range(2):
            out_copy(k, p).wait()


def body(records, band_gain, pair_mask):
    rec = records.reshape(WL, ROWS, L)
    any_space = pl.BlockSpec(memory_space=pl.ANY)
    vmem = pl.BlockSpec(memory_space=pltpu.VMEM)
    smem = pl.BlockSpec(memory_space=pltpu.SMEM)
    dma = pltpu.SemaphoreType.DMA
    sums = pl.pallas_call(
        kernel,
        out_shape=jax.ShapeDtypeStruct((5, BS, BS, 2, NB), F32),
        in_specs=[any_space, any_space, vmem, vmem, vmem, vmem, smem],
        out_specs=any_space,
        scratch_shapes=[
            pltpu.VMEM((2, ROWS, L), F32),
            pltpu.VMEM((2, 3 * L // 4, 512), BF16),
            pltpu.VMEM((2 * ROWS, L), BF16),
            pltpu.VMEM((ROWS, 2 * EXT), F32),
            pltpu.VMEM((2 * ROWS, EXT), BF16),
            pltpu.VMEM((2 * ROWS, EXT), F32),
            pltpu.VMEM((2 * ROWS, EXT), BF16),
            pltpu.VMEM((16, EXT), F32),
            pltpu.VMEM((WL, ROWS, 2 * NB), BF16),
            pltpu.VMEM((5, WL, NTM, BS, 2 * NB), BF16),
            pltpu.VMEM((2, WL, NTM, BS, 2 * NB), F32),
            pltpu.VMEM((5, BS, 2, BS, NB), F32),
            pltpu.VMEM((2, 3, BS, 2, BS, 128), BF16),
            pltpu.VMEM((2, 3, BS, 2, BS, 128), BF16),
            dma((2,)),
            dma,
            dma((WL, NTM)),
            dma((WL, NTM)),
            dma((WL, NTM)),
            dma((WL, NTM)),
            dma((WL, 3, 2)),
            dma((WL, 3, 2)),
            dma((WL, 3, 2)),
            dma((WL, 3, 2)),
            dma((2, 3)),
            dma((2, 3)),
            dma((5, 2)),
        ],
        compiler_params=pltpu.CompilerParams(
            collective_id=0, has_side_effects=True, vmem_limit_bytes=58 << 20
        ),
        cost_estimate=pl.CostEstimate(
            flops=10**10, bytes_accessed=30 * 10**6, transcendentals=10**6
        ),
    )(
        rec,
        jnp.asarray(dft_tables()),
        jnp.asarray(smoother_table()),
        jnp.asarray(order_table()),
        jnp.asarray(hann_row()),
        band_gain,
        pair_mask,
    )
    return sums[None]


def solution(mesh):
    placed = (P("tm", None, "chan", None, None), P(), P(("tm", "chan"), None))
    return jax.shard_map(
        body,
        mesh=mesh,
        in_specs=placed,
        out_specs=P(("tm", "chan"), None, None, None, None, None),
        check_vma=False,
    )
```

```python
import jax
import jax.numpy as jnp
import ml_dtypes
import numpy as np
from jax import lax
from jax.experimental import pallas as pl
from jax.experimental.pallas import tpu as pltpu
from jax.sharding import PartitionSpec as P

L = 4096
F0 = 8
HW = 64
NB = 384
EXT = NB + 2 * HW
NTM = 16
NCHAN = 8
NBLK = NTM * NCHAN
BS = 16
WL = 4
ROWS = NTM * BS
MESH = pl.DeviceIdType.MESH
F32 = jnp.float32
BF16 = jnp.bfloat16
OWN, ABOVE, X1, X2, BELOW = range(5)


def bin_order():
    j = np.arange(EXT)
    return np.concatenate([j[j % 4 == 0], j[j % 4 == 2], j[j % 2 == 1]])


def dft_tables():
    order = bin_order()

    def parts(samples, bins):
        phase = (np.arange(samples)[:, None] * (F0 + bins)[None, :] % L) * (2 * np.pi / L)
        return np.cos(phase) / 64.0, -np.sin(phase) / 64.0

    quarter = EXT // 4
    even = []
    for r in range(2):
        even += parts(L // 4, order[r * quarter : (r + 1) * quarter])
    even = np.concatenate(even, axis=1)
    odd = np.concatenate(parts(L // 2, order[2 * quarter :]), axis=1)

    def split(table):
        high = table.astype(ml_dtypes.bfloat16)
        low = (table - high.astype(np.float64)).astype(ml_dtypes.bfloat16)
        return np.stack([high, low])

    return np.concatenate([split(even), split(odd)], axis=1)


def smoother_table():
    order = bin_order()
    lower = order - HW
    covered = (order[:, None] >= lower[None, :]) & (order[:, None] <= lower[None, :] + 2 * HW)
    return covered.astype(ml_dtypes.bfloat16)


def order_table():
    order = bin_order()
    return (order[:, None] == np.arange(NB)[None, :] + HW).astype(ml_dtypes.bfloat16)


def hann_row():
    n = np.arange(L)
    return (0.5 - 0.5 * np.cos(2 * np.pi * n / L)).astype(np.float32)[None, :]


def device_of(block):
    wrapped = lax.rem(block + NBLK, NBLK)
    return (wrapped // NCHAN, lax.rem(wrapped, NCHAN))


def kernel(
    rec,
    tab_hbm,
    smooth,
    perm,
    hann,
    gain,
    mask,
    out,
    xbuf,
    tab,
    fold,
    spec,
    pw,
    lev,
    wh,
    gperm,
    send,
    blocks,
    wide,
    acc,
    give,
    take,
    rec_sem,
    tab_sem,
    a2a_s,
    a2a_r,
    dup_s,
    dup_r,
    ring_s,
    ring_r,
    sib_s,
    sib_r,
    give_s,
    give_r,
    out_sem,
):
    t = lax.axis_index("tm")
    c = lax.axis_index("chan")
    block = t * NCHAN + c
    core = lax.rem(c, 2)
    before = device_of(block - 2)
    after = device_of(block + 2)
    sibling = (t, c + 1 - 2 * core)
    first = c < 2
    last = c >= NCHAN - 2
    shift = jnp.where(first, 1, -1)
    round_corner = lax.rem(c + 6 * shift + NCHAN, NCHAN)
    dup_slot = jnp.where(first, ABOVE, BELOW)

    def rec_copy(w):
        slot = lax.rem(w, 2)
        return pltpu.make_async_copy(rec.at[w], xbuf.at[slot], rec_sem.at[slot])

    tab_copy = pltpu.make_async_copy(tab_hbm, tab, tab_sem)
    rec_copy(0).start()
    tab_copy.start()
    rec_copy(1).start()

    barrier = pltpu.get_barrier_semaphore()
    for d in range(1, NTM):
        pl.semaphore_signal(
            barrier, inc=1, device_id=(lax.rem(t + d, NTM), c), device_id_type=MESH
        )
    pl.semaphore_signal(barrier, inc=1, device_id=sibling, device_id_type=MESH)

    @pl.when(jnp.logical_not(first))
    def _():
        pl.semaphore_signal(barrier, inc=1, device_id=before, device_id_type=MESH)

    @pl.when(jnp.logical_not(last))
    def _():
        pl.semaphore_signal(barrier, inc=1, device_id=after, device_id_type=MESH)

    @pl.when(first | last)
    def _():
        for d in range(NTM):
            pl.semaphore_signal(
                barrier, inc=1, device_id=(lax.rem(t + d, NTM), round_corner), device_id_type=MESH
            )

    def clear(i, _):
        acc[i // 16, lax.rem(i, 16)] = jnp.zeros((2, BS, NB), F32)
        return 0

    lax.fori_loop(0, 80, clear, 0)

    rest = jnp.broadcast_to(gain[...].reshape(1, NB), (16, NB))
    total = jnp.zeros((16, EXT), F32)
    for _ in range(3):
        piece = rest.astype(BF16)
        rest = rest - piece.astype(F32)
        total += lax.dot_general(
            piece, perm[...], (((1,), (1,)), ((), ())), preferred_element_type=F32
        )
    gperm[...] = total

    def a2a_copy(w, d):
        q = lax.rem(t + d, NTM)
        return pltpu.make_async_remote_copy(
            src_ref=send.at[w, pl.ds(pl.multiple_of(q * BS, BS), BS)],
            dst_ref=blocks.at[OWN, w, t],
            send_sem=a2a_s.at[w, d],
            recv_sem=a2a_r.at[w, d],
            device_id=(q, c),
            device_id_type=MESH,
        )

    def dup_copy(w, d):
        r = lax.rem(t + d, NTM)
        q = lax.rem(r + shift + NTM, NTM)
        return pltpu.make_async_remote_copy(
            src_ref=send.at[w, pl.ds(pl.multiple_of(q * BS, BS), BS)],
            dst_ref=blocks.at[dup_slot, w, t],
            send_sem=dup_s.at[w, d],
            recv_sem=dup_r.at[w, d],
            device_id=(r, round_corner),
            device_id_type=MESH,
        )

    def bins_of(ref, slot, w, f):
        return ref.at[slot, w, :, :, pl.ds(pl.multiple_of(f * 256, 256), 256)]

    def ring_copy(w, up, f):
        return pltpu.make_async_remote_copy(
            src_ref=bins_of(blocks, OWN, w, f),
            dst_ref=bins_of(blocks, ABOVE if up else BELOW, w, f),
            send_sem=ring_s.at[w, f, up],
            recv_sem=ring_r.at[w, f, up],
            device_id=before if up else after,
            device_id_type=MESH,
        )

    def sib_copy(w, source, slot, f):
        return pltpu.make_async_remote_copy(
            src_ref=bins_of(blocks, source, w, f),
            dst_ref=bins_of(blocks, slot, w, f),
            send_sem=sib_s.at[w, f, slot - X1],
            recv_sem=sib_r.at[w, f, slot - X1],
            device_id=sibling,
            device_id_type=MESH,
        )

    def widen(which, source, w, f):
        at = pl.ds(pl.multiple_of(f * 256, 256), 256)

        def one(i, _):
            wide[which, w, i, :, at] = blocks[source, w, i, :, at].astype(F32)
            return 0

        lax.fori_loop(0, NTM, one, 0, unroll=4)

    def spread(w):
        for d in range(1, NTM):
            a2a_copy(w, d).wait_recv()
        for f in range(3):

            @pl.when(jnp.logical_not(first))
            def _():
                ring_copy(w, 1, f).start()

            @pl.when(jnp.logical_not(last))
            def _():
                ring_copy(w, 0, f).start()

            @pl.when(core == 1)
            def _():
                sib_copy(w, OWN, X1, f).start()

        for f in range(3):
            widen(0, OWN, w, f)

    def transform(w, _):
        slot = lax.rem(w, 2)
        rec_copy(w).wait()

        def fold_rows(i, _):
            rows = pl.ds(pl.multiple_of(i * 16, 16), 16)
            low_rows = pl.ds(pl.multiple_of(ROWS + i * 16, 16), 16)

            def put(value, at):
                high = value.astype(BF16)
                fold[rows, at : at + 128] = high
                fold[low_rows, at : at + 128] = (value - high.astype(F32)).astype(BF16)

            for p in range(0, L // 4, 128):
                x0, x1, x2, x3 = (
                    xbuf[slot, rows, s + p : s + p + 128] * hann[:, s + p : s + p + 128]
                    for s in range(0, L, L // 4)
                )
                u, v = x0 + x2, x1 + x3
                put(u + v, p)
                put(u - v, L // 4 + p)
                put(x0 - x2, L // 2 + p)
                put(x1 - x3, 3 * L // 4 + p)
            return 0

        lax.fori_loop(0, ROWS // 16, fold_rows, 0)

        @pl.when(w + 2 < WL)
        def _():
            rec_copy(w + 2).start()

        @pl.when(w == 0)
        def _():
            tab_copy.wait()

        def product(at, length, trow, tcol, col):
            both = jnp.dot(
                fold[:, at : at + length],
                tab[0, trow : trow + length, tcol : tcol + 256],
                preferred_element_type=F32,
            )
            low = jnp.dot(
                fold[:ROWS, at : at + length],
                tab[1, trow : trow + length, tcol : tcol + 256],
                preferred_element_type=F32,
            )
            spec[:, col : col + 256] = both[:ROWS] + (both[ROWS:] + low)

        product(0, L // 4, 0, 0, 0)
        product(L // 4, L // 4, 0, 256, 256)
        product(L // 2, L // 2, L // 4, 0, 512)
        product(L // 2, L // 2, L // 4, 256, 768)

        def spectrum(rows):
            re = jnp.concatenate([spec[rows, 0:128], spec[rows, 256:384], spec[rows, 512:768]], 1)
            im = jnp.concatenate([spec[rows, 128:256], spec[rows, 384:512], spec[rows, 768:1024]], 1)
            return re, im

        def power_rows(i, _):
            rows = pl.ds(pl.multiple_of(i * 16, 16), 16)
            re, im = spectrum(rows)
            power = re * re + im * im
            high = power.astype(BF16)
            pw[rows] = high
            pw[pl.ds(pl.multiple_of(ROWS + i * 16, 16), 16)] = (power - high.astype(F32)).astype(BF16)
            return 0

        lax.fori_loop(0, ROWS // 16, power_rows, 0)
        lev[...] = jnp.dot(pw[...], smooth[...], preferred_element_type=F32)

        def white_rows(i, _):
            rows = pl.ds(pl.multiple_of(i * 16, 16), 16)
            low_rows = pl.ds(pl.multiple_of(ROWS + i * 16, 16), 16)
            level = (lev[rows] + lev[low_rows]) / (2 * HW + 1)
            factor = gperm[...] * lax.rsqrt(level + 1e-6)
            re, im = spectrum(rows)
            wh[rows] = (re * factor).astype(BF16)
            wh[low_rows] = (im * factor).astype(BF16)
            return 0

        lax.fori_loop(0, ROWS // 16, white_rows, 0)
        white = jnp.dot(wh[...], perm[...], preferred_element_type=F32)
        for f in range(3):
            at = f * 256
            send[w, :, at : at + 128] = white[:ROWS, f * 128 : f * 128 + 128].astype(BF16)
            send[w, :, at + 128 : at + 256] = white[ROWS:, f * 128 : f * 128 + 128].astype(BF16)

        @pl.when((w == 0) & jnp.logical_not(first | last))
        def _():
            pl.semaphore_wait(barrier, NTM - 1 + 3)

        @pl.when((w == 0) & (first | last))
        def _():
            pl.semaphore_wait(barrier, NTM - 1 + 2 + NTM)

        for d in range(1, NTM):
            a2a_copy(w, d).start()
        blocks[OWN, w, t] = send[w, pl.ds(pl.multiple_of(t * BS, BS), BS)]

        @pl.when(w > 0)
        def _():
            spread(w - 1)

        @pl.when((w > 0) & (first | last))
        def _():
            for d in range(NTM):
                dup_copy(w - 1, d).start()

        return 0

    lax.fori_loop(0, WL, transform, 0)

    @pl.when(first | last)
    def _():
        for d in range(NTM):
            dup_copy(WL - 1, d).start()

    def correlate(k, left, right, w, f):
        re_at = pl.ds(pl.multiple_of(f * 256, 128), 128)
        im_at = pl.ds(pl.multiple_of(f * 256 + 128, 128), 128)
        at = pl.ds(pl.multiple_of(f * 128, 128), 128)
        for half in range(2):
            mine = range(half * 8, half * 8 + 8)
            start = tuple(acc[k, a, p, :, at] for a in mine for p in range(2))

            def window(n, sums):
                cr = blocks[right, w, n, :, re_at].astype(F32)
                ci = blocks[right, w, n, :, im_at].astype(F32)
                new = []
                for i, a in enumerate(mine):
                    ar = wide[left, w, n, a : a + 1, re_at]
                    ai = wide[left, w, n, a : a + 1, im_at]
                    new.append((sums[2 * i] + ar * cr) + ai * ci)
                    new.append((sums[2 * i + 1] + ai * cr) - ar * ci)
                return tuple(new)

            sums = lax.fori_loop(0, NTM, window, start, unroll=8)
            for i, a in enumerate(mine):
                for p in range(2):
                    acc[k, a, p, :, at] = sums[2 * i + p]

    def selfs(i, _):
        correlate(0, 0, OWN, i // 3, lax.rem(i, 3))
        return 0

    lax.fori_loop(0, 3 * (WL - 1), selfs, 0)
    spread(WL - 1)
    lax.fori_loop(3 * (WL - 1), 3 * WL, selfs, 0)

    def give_copy(i, f):
        return pltpu.make_async_remote_copy(
            src_ref=give.at[i, f],
            dst_ref=take.at[i, f],
            send_sem=give_s.at[i, f],
            recv_sem=give_r.at[i, f],
            device_id=before,
            device_id_type=MESH,
        )

    def hand_over(i, k, f):
        at = pl.ds(pl.multiple_of(f * 128, 128), 128)

        def one(a, _):
            give[i, f, a] = acc[k, a, :, :, at].astype(BF16)
            return 0

        lax.fori_loop(0, BS, one, 0, unroll=4)
        give_copy(i, f).start()

    left3 = core
    right3 = X2 - core

    def partners(i, _):
        w = i // 3
        f = lax.rem(i, 3)

        @pl.when(jnp.logical_not(last))
        def _():
            ring_copy(w, 1, f).wait_recv()

        @pl.when(jnp.logical_not(first))
        def _():
            ring_copy(w, 0, f).wait_recv()

        @pl.when((first | last) & (f == 0))
        def _():
            for d in range(NTM):
                dup_copy(w, d).wait_recv()

        @pl.when(core == 0)
        def _():
            sib_copy(w, ABOVE, X1, f).start()

        @pl.when(core == 1)
        def _():
            sib_copy(w, ABOVE, X2, f).start()

        widen(1, BELOW, w, f)
        correlate(4, 1, ABOVE, w, f)

        @pl.when(w == WL - 1)
        def _():
            hand_over(0, 4, f)

        correlate(2, 0, ABOVE, w, f)
        sib_copy(w, OWN, X1, f).wait_recv()

        @pl.when(core == 0)
        def _():
            sib_copy(w, OWN, X2, f).wait_recv()

        correlate(3, left3, right3, w, f)

        @pl.when((w == WL - 1) & (core == 1))
        def _():
            hand_over(1, 3, f)

        correlate(1, 0, X1, w, f)
        return 0

    def out_copy(k, p):
        return pltpu.make_async_copy(acc.at[k, :, p], out.at[k, :, p], out_sem.at[k, p])

    def weight_of(k):
        inside = (block + k < NBLK).astype(F32)
        return mask[0, k].astype(F32) * inside * (1.0 / 64.0)

    def finish(k):
        weight = weight_of(k)

        def one(a, _):
            acc[k, a] = acc[k, a] * weight
            return 0

        lax.fori_loop(0, BS, one, 0, unroll=2)
        for p in range(2):
            out_copy(k, p).start()

    def finish_taken(k, i):
        weight = weight_of(k)
        for f in range(3):
            give_copy(i, f).wait_recv()

            def one(a, _):
                acc[k, a, :, :, f * 128 : f * 128 + 128] = take[i, f, a].astype(F32) * weight
                return 0

            lax.fori_loop(0, BS, one, 0, unroll=4)
        for p in range(2):
            out_copy(k, p).start()

    finish(0)
    lax.fori_loop(0, 3 * WL, partners, 0)

    finish(2)
    finish(1)

    @pl.when(core == 0)
    def _():
        finish(3)

    finish_taken(4, 0)

    @pl.when(core == 1)
    def _():
        finish_taken(3, 1)

    def drain(i, _):
        w = i // 3
        f = lax.rem(i, 3)

        @pl.when(f == 0)
        def _():
            for d in range(1, NTM):
                a2a_copy(w, d).wait_send()

        @pl.when((first | last) & (f == 0))
        def _():
            for d in range(NTM):
                dup_copy(w, d).wait_send()

        @pl.when(jnp.logical_not(first))
        def _():
            ring_copy(w, 1, f).wait_send()

        @pl.when(jnp.logical_not(last))
        def _():
            ring_copy(w, 0, f).wait_send()

        @pl.when(core == 0)
        def _():
            sib_copy(w, ABOVE, X1, f).wait_send()

        @pl.when(core == 1)
        def _():
            sib_copy(w, OWN, X1, f).wait_send()
            sib_copy(w, ABOVE, X2, f).wait_send()

        return 0

    lax.fori_loop(0, 3 * WL, drain, 0)
    for f in range(3):
        give_copy(0, f).wait_send()

        @pl.when(core == 1)
        def _():
            give_copy(1, f).wait_send()

    for k in range(5):
        for p in range(2):
            out_copy(k, p).wait()


def place_kernel(sums, out, held, in_sem, out_sem):
    def take_in(k):
        return pltpu.make_async_copy(sums.at[k], held.at[k], in_sem.at[k])

    def put_out(k, p):
        return pltpu.make_async_copy(held.at[k, :, p], out.at[k, :, :, p], out_sem.at[k, p])

    for k in range(5):
        take_in(k).start()
    for k in range(5):
        take_in(k).wait()
        for p in range(2):
            put_out(k, p).start()
    for k in range(5):
        for p in range(2):
            put_out(k, p).wait()


def body(records, band_gain, pair_mask):
    rec = records.reshape(WL, ROWS, L)
    any_space = pl.BlockSpec(memory_space=pl.ANY)
    vmem = pl.BlockSpec(memory_space=pltpu.VMEM)
    smem = pl.BlockSpec(memory_space=pltpu.SMEM)
    dma = pltpu.SemaphoreType.DMA
    sums = pl.pallas_call(
        kernel,
        out_shape=jax.ShapeDtypeStruct((5, BS, 2, BS, NB), F32),
        in_specs=[any_space, any_space, vmem, vmem, vmem, vmem, smem],
        out_specs=any_space,
        scratch_shapes=[
            pltpu.VMEM((2, ROWS, L), F32),
            pltpu.VMEM((2, 3 * L // 4, 512), BF16),
            pltpu.VMEM((2 * ROWS, L), BF16),
            pltpu.VMEM((ROWS, 2 * EXT), F32),
            pltpu.VMEM((2 * ROWS, EXT), BF16),
            pltpu.VMEM((2 * ROWS, EXT), F32),
            pltpu.VMEM((2 * ROWS, EXT), BF16),
            pltpu.VMEM((16, EXT), F32),
            pltpu.VMEM((WL, ROWS, 2 * NB), BF16),
            pltpu.VMEM((5, WL, NTM, BS, 2 * NB), BF16),
            pltpu.VMEM((2, WL, NTM, BS, 2 * NB), F32),
            pltpu.VMEM((5, BS, 2, BS, NB), F32),
            pltpu.VMEM((2, 3, BS, 2, BS, 128), BF16),
            pltpu.VMEM((2, 3, BS, 2, BS, 128), BF16),
            dma((2,)),
            dma,
            dma((WL, NTM)),
            dma((WL, NTM)),
            dma((WL, NTM)),
            dma((WL, NTM)),
            dma((WL, 3, 2)),
            dma((WL, 3, 2)),
            dma((WL, 3, 2)),
            dma((WL, 3, 2)),
            dma((2, 3)),
            dma((2, 3)),
            dma((5, 2)),
        ],
        compiler_params=pltpu.CompilerParams(
            collective_id=0, has_side_effects=True, vmem_limit_bytes=58 << 20
        ),
        cost_estimate=pl.CostEstimate(
            flops=10**10, bytes_accessed=30 * 10**6, transcendentals=10**6
        ),
    )(
        rec,
        jnp.asarray(dft_tables()),
        jnp.asarray(smoother_table()),
        jnp.asarray(order_table()),
        jnp.asarray(hann_row()),
        band_gain,
        pair_mask,
    )
    stacks = pl.pallas_call(
        place_kernel,
        out_shape=jax.ShapeDtypeStruct((5, BS, BS, 2, NB), F32),
        in_specs=[any_space],
        out_specs=any_space,
        scratch_shapes=[pltpu.VMEM((5, BS, 2, BS, NB), F32), dma((5,)), dma((5, 2))],
        cost_estimate=pl.CostEstimate(flops=0, bytes_accessed=8 * 10**6, transcendentals=0),
    )(sums)
    return stacks[None]


def solution(mesh):
    placed = (P("tm", None, "chan", None, None), P(), P(("tm", "chan"), None))
    return jax.shard_map(
        body,
        mesh=mesh,
        in_specs=placed,
        out_specs=P(("tm", "chan"), None, None, None, None, None),
        check_vma=False,
    )
```

```python
import jax
import jax.numpy as jnp
import ml_dtypes
import numpy as np
from jax import lax
from jax.experimental import pallas as pl
from jax.experimental.pallas import tpu as pltpu
from jax.sharding import PartitionSpec as P

L = 4096
F0 = 8
HW = 64
NB = 384
EXT = NB + 2 * HW
NTM = 16
NCHAN = 8
NBLK = NTM * NCHAN
BS = 16
WL = 4
ROWS = NTM * BS
MESH = pl.DeviceIdType.MESH
F32 = jnp.float32
BF16 = jnp.bfloat16
OWN, ABOVE, X1, X2, BELOW = range(5)


def bin_order():
    j = np.arange(EXT)
    return np.concatenate([j[j % 4 == 0], j[j % 4 == 2], j[j % 2 == 1]])


def dft_tables():
    order = bin_order()

    def parts(samples, bins):
        phase = (np.arange(samples)[:, None] * (F0 + bins)[None, :] % L) * (2 * np.pi / L)
        return np.cos(phase) / 64.0, -np.sin(phase) / 64.0

    quarter = EXT // 4
    even = []
    for r in range(2):
        even += parts(L // 4, order[r * quarter : (r + 1) * quarter])
    even = np.concatenate(even, axis=1)
    odd = np.concatenate(parts(L // 2, order[2 * quarter :]), axis=1)

    def split(table):
        high = table.astype(ml_dtypes.bfloat16)
        low = (table - high.astype(np.float64)).astype(ml_dtypes.bfloat16)
        return np.stack([high, low])

    return np.concatenate([split(even), split(odd)], axis=1)


def smoother_table():
    order = bin_order()
    lower = order - HW
    covered = (order[:, None] >= lower[None, :]) & (order[:, None] <= lower[None, :] + 2 * HW)
    return covered.astype(ml_dtypes.bfloat16)


def order_table():
    order = bin_order()
    return (order[:, None] == np.arange(NB)[None, :] + HW).astype(ml_dtypes.bfloat16)


def hann_row():
    n = np.arange(L)
    return (0.5 - 0.5 * np.cos(2 * np.pi * n / L)).astype(np.float32)[None, :]


def device_of(block):
    wrapped = lax.rem(block + NBLK, NBLK)
    return (wrapped // NCHAN, lax.rem(wrapped, NCHAN))


def kernel(
    rec,
    tab_hbm,
    smooth,
    perm,
    hann,
    gain,
    mask,
    out,
    xbuf,
    tab,
    fold,
    spec,
    pw,
    lev,
    wh,
    gperm,
    send,
    blocks,
    wide,
    other,
    acc,
    give,
    take,
    rec_sem,
    tab_sem,
    a2a_s,
    a2a_r,
    dup_s,
    dup_r,
    ring_s,
    ring_r,
    sib_s,
    sib_r,
    give_s,
    give_r,
    out_sem,
):
    t = lax.axis_index("tm")
    c = lax.axis_index("chan")
    block = t * NCHAN + c
    core = lax.rem(c, 2)
    before = device_of(block - 2)
    after = device_of(block + 2)
    sibling = (t, c + 1 - 2 * core)
    first = c < 2
    last = c >= NCHAN - 2
    shift = jnp.where(first, 1, -1)
    round_corner = lax.rem(c + 6 * shift + NCHAN, NCHAN)
    dup_slot = jnp.where(first, ABOVE, BELOW)

    def rec_copy(w):
        slot = lax.rem(w, 2)
        return pltpu.make_async_copy(rec.at[w], xbuf.at[slot], rec_sem.at[slot])

    tab_copy = pltpu.make_async_copy(tab_hbm, tab, tab_sem)
    rec_copy(0).start()
    tab_copy.start()
    rec_copy(1).start()

    barrier = pltpu.get_barrier_semaphore()
    for d in range(1, NTM):
        pl.semaphore_signal(
            barrier, inc=1, device_id=(lax.rem(t + d, NTM), c), device_id_type=MESH
        )
    pl.semaphore_signal(barrier, inc=1, device_id=sibling, device_id_type=MESH)

    @pl.when(jnp.logical_not(first))
    def _():
        pl.semaphore_signal(barrier, inc=1, device_id=before, device_id_type=MESH)

    @pl.when(jnp.logical_not(last))
    def _():
        pl.semaphore_signal(barrier, inc=1, device_id=after, device_id_type=MESH)

    @pl.when(first | last)
    def _():
        for d in range(NTM):
            pl.semaphore_signal(
                barrier, inc=1, device_id=(lax.rem(t + d, NTM), round_corner), device_id_type=MESH
            )

    def clear(i, _):
        acc[i // 16, lax.rem(i, 16)] = jnp.zeros((2, BS, NB), F32)
        return 0

    lax.fori_loop(0, 80, clear, 0)

    rest = jnp.broadcast_to(gain[...].reshape(1, NB), (16, NB))
    total = jnp.zeros((16, EXT), F32)
    for _ in range(3):
        piece = rest.astype(BF16)
        rest = rest - piece.astype(F32)
        total += lax.dot_general(
            piece, perm[...], (((1,), (1,)), ((), ())), preferred_element_type=F32
        )
    gperm[...] = total

    def a2a_copy(w, d):
        q = lax.rem(t + d, NTM)
        return pltpu.make_async_remote_copy(
            src_ref=send.at[w, pl.ds(pl.multiple_of(q * BS, BS), BS)],
            dst_ref=blocks.at[OWN, w, t],
            send_sem=a2a_s.at[w, d],
            recv_sem=a2a_r.at[w, d],
            device_id=(q, c),
            device_id_type=MESH,
        )

    def dup_copy(w, d):
        r = lax.rem(t + d, NTM)
        q = lax.rem(r + shift + NTM, NTM)
        return pltpu.make_async_remote_copy(
            src_ref=send.at[w, pl.ds(pl.multiple_of(q * BS, BS), BS)],
            dst_ref=blocks.at[dup_slot, w, t],
            send_sem=dup_s.at[w, d],
            recv_sem=dup_r.at[w, d],
            device_id=(r, round_corner),
            device_id_type=MESH,
        )

    def bins_of(ref, slot, w, f):
        return ref.at[slot, w, :, :, pl.ds(pl.multiple_of(f * 256, 256), 256)]

    def ring_copy(w, up, f):
        return pltpu.make_async_remote_copy(
            src_ref=bins_of(blocks, OWN, w, f),
            dst_ref=bins_of(blocks, ABOVE if up else BELOW, w, f),
            send_sem=ring_s.at[w, f, up],
            recv_sem=ring_r.at[w, f, up],
            device_id=before if up else after,
            device_id_type=MESH,
        )

    def sib_copy(w, source, slot, f):
        return pltpu.make_async_remote_copy(
            src_ref=bins_of(blocks, source, w, f),
            dst_ref=bins_of(blocks, slot, w, f),
            send_sem=sib_s.at[w, f, slot - X1],
            recv_sem=sib_r.at[w, f, slot - X1],
            device_id=sibling,
            device_id_type=MESH,
        )

    def widen(which, source, w, f):
        at = pl.ds(pl.multiple_of(f * 256, 256), 256)
        to = pl.multiple_of(f * 384, 384)

        def one(i, _):
            both = blocks[source, w, i, :, at].astype(F32)
            wide[which, w, i, :, pl.ds(to, 256)] = both
            wide[which, w, i, :, pl.ds(to + 256, 128)] = both[:, :128] + both[:, 128:]
            return 0

        lax.fori_loop(0, NTM, one, 0, unroll=4)

    def widen_other(slot, w, f):
        at = pl.ds(pl.multiple_of(f * 256, 256), 256)

        def one(i, _):
            other[slot - ABOVE, i] = blocks[slot, w, i, :, at].astype(F32)
            return 0

        lax.fori_loop(0, NTM, one, 0, unroll=4)

    def spread(w):
        for d in range(1, NTM):
            a2a_copy(w, d).wait_recv()
        for f in range(3):

            @pl.when(jnp.logical_not(first))
            def _():
                ring_copy(w, 1, f).start()

            @pl.when(jnp.logical_not(last))
            def _():
                ring_copy(w, 0, f).start()

            @pl.when(core == 1)
            def _():
                sib_copy(w, OWN, X1, f).start()

        for f in range(3):
            widen(0, OWN, w, f)

    def transform(w, _):
        slot = lax.rem(w, 2)
        rec_copy(w).wait()

        def fold_rows(i, _):
            rows = pl.ds(pl.multiple_of(i * 16, 16), 16)
            low_rows = pl.ds(pl.multiple_of(ROWS + i * 16, 16), 16)

            def put(value, at):
                high = value.astype(BF16)
                fold[rows, at : at + 128] = high
                fold[low_rows, at : at + 128] = (value - high.astype(F32)).astype(BF16)

            for p in range(0, L // 4, 128):
                x0, x1, x2, x3 = (
                    xbuf[slot, rows, s + p : s + p + 128] * hann[:, s + p : s + p + 128]
                    for s in range(0, L, L // 4)
                )
                u, v = x0 + x2, x1 + x3
                put(u + v, p)
                put(u - v, L // 4 + p)
                put(x0 - x2, L // 2 + p)
                put(x1 - x3, 3 * L // 4 + p)
            return 0

        lax.fori_loop(0, ROWS // 16, fold_rows, 0)

        @pl.when(w + 2 < WL)
        def _():
            rec_copy(w + 2).start()

        @pl.when(w == 0)
        def _():
            tab_copy.wait()

        def product(at, length, trow, tcol, col):
            both = jnp.dot(
                fold[:, at : at + length],
                tab[0, trow : trow + length, tcol : tcol + 256],
                preferred_element_type=F32,
            )
            low = jnp.dot(
                fold[:ROWS, at : at + length],
                tab[1, trow : trow + length, tcol : tcol + 256],
                preferred_element_type=F32,
            )
            spec[:, col : col + 256] = both[:ROWS] + (both[ROWS:] + low)

        product(0, L // 4, 0, 0, 0)
        product(L // 4, L // 4, 0, 256, 256)
        product(L // 2, L // 2, L // 4, 0, 512)
        product(L // 2, L // 2, L // 4, 256, 768)

        def spectrum(rows):
            re = jnp.concatenate([spec[rows, 0:128], spec[rows, 256:384], spec[rows, 512:768]], 1)
            im = jnp.concatenate([spec[rows, 128:256], spec[rows, 384:512], spec[rows, 768:1024]], 1)
            return re, im

        def power_rows(i, _):
            rows = pl.ds(pl.multiple_of(i * 16, 16), 16)
            re, im = spectrum(rows)
            power = re * re + im * im
            high = power.astype(BF16)
            pw[rows] = high
            pw[pl.ds(pl.multiple_of(ROWS + i * 16, 16), 16)] = (power - high.astype(F32)).astype(BF16)
            return 0

        lax.fori_loop(0, ROWS // 16, power_rows, 0)
        lev[...] = jnp.dot(pw[...], smooth[...], preferred_element_type=F32)

        def white_rows(i, _):
            rows = pl.ds(pl.multiple_of(i * 16, 16), 16)
            low_rows = pl.ds(pl.multiple_of(ROWS + i * 16, 16), 16)
            level = (lev[rows] + lev[low_rows]) / (2 * HW + 1)
            factor = gperm[...] * lax.rsqrt(level + 1e-6)
            re, im = spectrum(rows)
            wh[rows] = (re * factor).astype(BF16)
            wh[low_rows] = (im * factor).astype(BF16)
            return 0

        lax.fori_loop(0, ROWS // 16, white_rows, 0)
        white = jnp.dot(wh[...], perm[...], preferred_element_type=F32)
        for f in range(3):
            at = f * 256
            send[w, :, at : at + 128] = white[:ROWS, f * 128 : f * 128 + 128].astype(BF16)
            send[w, :, at + 128 : at + 256] = white[ROWS:, f * 128 : f * 128 + 128].astype(BF16)

        @pl.when((w == 0) & jnp.logical_not(first | last))
        def _():
            pl.semaphore_wait(barrier, NTM - 1 + 3)

        @pl.when((w == 0) & (first | last))
        def _():
            pl.semaphore_wait(barrier, NTM - 1 + 2 + NTM)

        for d in range(1, NTM):
            a2a_copy(w, d).start()
        blocks[OWN, w, t] = send[w, pl.ds(pl.multiple_of(t * BS, BS), BS)]

        @pl.when(w > 0)
        def _():
            spread(w - 1)

        @pl.when((w > 0) & (first | last))
        def _():
            for d in range(NTM):
                dup_copy(w - 1, d).start()

        return 0

    lax.fori_loop(0, WL, transform, 0)

    @pl.when(first | last)
    def _():
        for d in range(NTM):
            dup_copy(WL - 1, d).start()

    def correlate(k, left, right, w, f):
        re_at = pl.ds(pl.multiple_of(f * 384, 128), 128)
        im_at = pl.ds(pl.multiple_of(f * 384 + 128, 128), 128)
        sum_at = pl.ds(pl.multiple_of(f * 384 + 256, 128), 128)
        at = pl.ds(pl.multiple_of(f * 128, 128), 128)
        zero = jnp.zeros((BS, 128), F32)
        for part in range(4):
            mine = range(part * 4, part * 4 + 4)

            def window(n, sums):
                if right is None:
                    cr = wide[0, w, n, :, re_at]
                    ci = wide[0, w, n, :, im_at]
                else:
                    cr = other[right, n, :, :128]
                    ci = other[right, n, :, 128:]
                plus, minus = cr + ci, cr - ci
                new = []
                for i, a in enumerate(mine):
                    new.append(sums[3 * i] + wide[left, w, n, a : a + 1, sum_at] * cr)
                    new.append(sums[3 * i + 1] + wide[left, w, n, a : a + 1, re_at] * plus)
                    new.append(sums[3 * i + 2] + wide[left, w, n, a : a + 1, im_at] * minus)
                return tuple(new)

            sums = lax.fori_loop(0, NTM, window, (zero,) * 12, unroll=8)
            for i, a in enumerate(mine):
                acc[k, a, 0, :, at] += sums[3 * i] - sums[3 * i + 2]
                acc[k, a, 1, :, at] += sums[3 * i] - sums[3 * i + 1]

    def selfs(i, _):
        correlate(0, 0, None, i // 3, lax.rem(i, 3))
        return 0

    lax.fori_loop(0, 3 * (WL - 1), selfs, 0)
    spread(WL - 1)
    lax.fori_loop(3 * (WL - 1), 3 * WL, selfs, 0)

    def give_copy(i, f):
        return pltpu.make_async_remote_copy(
            src_ref=give.at[i, f],
            dst_ref=take.at[i, f],
            send_sem=give_s.at[i, f],
            recv_sem=give_r.at[i, f],
            device_id=before,
            device_id_type=MESH,
        )

    def hand_over(i, k, f):
        at = pl.ds(pl.multiple_of(f * 128, 128), 128)

        def one(a, _):
            give[i, f, a] = acc[k, a, :, :, at].astype(BF16)
            return 0

        lax.fori_loop(0, BS, one, 0, unroll=4)
        give_copy(i, f).start()

    left3 = core
    right3 = X2 - core - ABOVE

    def arrive(i):
        w = i // 3
        f = lax.rem(i, 3)

        @pl.when(jnp.logical_not(last))
        def _():
            ring_copy(w, 1, f).wait_recv()

        @pl.when(jnp.logical_not(first))
        def _():
            ring_copy(w, 0, f).wait_recv()

        @pl.when((first | last) & (f == 0))
        def _():
            for d in range(NTM):
                dup_copy(w, d).wait_recv()

        @pl.when(core == 0)
        def _():
            sib_copy(w, ABOVE, X1, f).start()

        @pl.when(core == 1)
        def _():
            sib_copy(w, ABOVE, X2, f).start()

        widen(1, BELOW, w, f)
        widen_other(ABOVE, w, f)
        correlate(4, 1, ABOVE - ABOVE, w, f)

        @pl.when(w == WL - 1)
        def _():
            hand_over(0, 4, f)

        correlate(2, 0, ABOVE - ABOVE, w, f)

    def use_shared(i):
        w = i // 3
        f = lax.rem(i, 3)
        sib_copy(w, OWN, X1, f).wait_recv()
        widen_other(X1, w, f)

        @pl.when(core == 0)
        def _():
            sib_copy(w, OWN, X2, f).wait_recv()
            widen_other(X2, w, f)

        correlate(3, left3, right3, w, f)

        @pl.when((w == WL - 1) & (core == 1))
        def _():
            hand_over(1, 3, f)

        correlate(1, 0, X1 - ABOVE, w, f)

    def partners(i, _):
        @pl.when(i < 3 * WL)
        def _():
            arrive(i)

        @pl.when(i > 0)
        def _():
            use_shared(i - 1)

        return 0

    def out_copy(k, p):
        return pltpu.make_async_copy(acc.at[k, :, p], out.at[k, :, p], out_sem.at[k, p])

    def weight_of(k):
        inside = (block + k < NBLK).astype(F32)
        return mask[0, k].astype(F32) * inside * (1.0 / 64.0)

    def finish(k):
        weight = weight_of(k)

        def one(a, _):
            acc[k, a] = acc[k, a] * weight
            return 0

        lax.fori_loop(0, BS, one, 0, unroll=2)
        for p in range(2):
            out_copy(k, p).start()

    def finish_taken(k, i):
        weight = weight_of(k)
        for f in range(3):
            give_copy(i, f).wait_recv()

            def one(a, _):
                acc[k, a, :, :, f * 128 : f * 128 + 128] = take[i, f, a].astype(F32) * weight
                return 0

            lax.fori_loop(0, BS, one, 0, unroll=4)
        for p in range(2):
            out_copy(k, p).start()

    finish(0)
    lax.fori_loop(0, 3 * WL + 1, partners, 0)

    finish(2)
    finish(1)

    @pl.when(core == 0)
    def _():
        finish(3)

    finish_taken(4, 0)

    @pl.when(core == 1)
    def _():
        finish_taken(3, 1)

    def drain(i, _):
        w = i // 3
        f = lax.rem(i, 3)

        @pl.when(f == 0)
        def _():
            for d in range(1, NTM):
                a2a_copy(w, d).wait_send()

        @pl.when((first | last) & (f == 0))
        def _():
            for d in range(NTM):
                dup_copy(w, d).wait_send()

        @pl.when(jnp.logical_not(first))
        def _():
            ring_copy(w, 1, f).wait_send()

        @pl.when(jnp.logical_not(last))
        def _():
            ring_copy(w, 0, f).wait_send()

        @pl.when(core == 0)
        def _():
            sib_copy(w, ABOVE, X1, f).wait_send()

        @pl.when(core == 1)
        def _():
            sib_copy(w, OWN, X1, f).wait_send()
            sib_copy(w, ABOVE, X2, f).wait_send()

        return 0

    lax.fori_loop(0, 3 * WL, drain, 0)
    for f in range(3):
        give_copy(0, f).wait_send()

        @pl.when(core == 1)
        def _():
            give_copy(1, f).wait_send()

    for k in range(5):
        for p in range(2):
            out_copy(k, p).wait()


def place_kernel(sums, out, held, in_sem, out_sem):
    def take_in(k):
        return pltpu.make_async_copy(sums.at[k], held.at[k], in_sem.at[k])

    def put_out(k, p):
        return pltpu.make_async_copy(held.at[k, :, p], out.at[k, :, :, p], out_sem.at[k, p])

    for k in range(5):
        take_in(k).start()
    for k in range(5):
        take_in(k).wait()
        for p in range(2):
            put_out(k, p).start()
    for k in range(5):
        for p in range(2):
            put_out(k, p).wait()


def body(records, band_gain, pair_mask):
    rec = records.reshape(WL, ROWS, L)
    any_space = pl.BlockSpec(memory_space=pl.ANY)
    vmem = pl.BlockSpec(memory_space=pltpu.VMEM)
    smem = pl.BlockSpec(memory_space=pltpu.SMEM)
    dma = pltpu.SemaphoreType.DMA
    sums = pl.pallas_call(
        kernel,
        out_shape=jax.ShapeDtypeStruct((5, BS, 2, BS, NB), F32),
        in_specs=[any_space, any_space, vmem, vmem, vmem, vmem, smem],
        out_specs=any_space,
        scratch_shapes=[
            pltpu.VMEM((2, ROWS, L), F32),
            pltpu.VMEM((2, 3 * L // 4, 512), BF16),
            pltpu.VMEM((2 * ROWS, L), BF16),
            pltpu.VMEM((ROWS, 2 * EXT), F32),
            pltpu.VMEM((2 * ROWS, EXT), BF16),
            pltpu.VMEM((2 * ROWS, EXT), F32),
            pltpu.VMEM((2 * ROWS, EXT), BF16),
            pltpu.VMEM((16, EXT), F32),
            pltpu.VMEM((WL, ROWS, 2 * NB), BF16),
            pltpu.VMEM((5, WL, NTM, BS, 2 * NB), BF16),
            pltpu.VMEM((2, WL, NTM, BS, 3 * NB), F32),
            pltpu.VMEM((3, NTM, BS, 256), F32),
            pltpu.VMEM((5, BS, 2, BS, NB), F32),
            pltpu.VMEM((2, 3, BS, 2, BS, 128), BF16),
            pltpu.VMEM((2, 3, BS, 2, BS, 128), BF16),
            dma((2,)),
            dma,
            dma((WL, NTM)),
            dma((WL, NTM)),
            dma((WL, NTM)),
            dma((WL, NTM)),
            dma((WL, 3, 2)),
            dma((WL, 3, 2)),
            dma((WL, 3, 2)),
            dma((WL, 3, 2)),
            dma((2, 3)),
            dma((2, 3)),
            dma((5, 2)),
        ],
        compiler_params=pltpu.CompilerParams(
            collective_id=0, has_side_effects=True, vmem_limit_bytes=58 << 20
        ),
        cost_estimate=pl.CostEstimate(
            flops=10**10, bytes_accessed=30 * 10**6, transcendentals=10**6
        ),
    )(
        rec,
        jnp.asarray(dft_tables()),
        jnp.asarray(smoother_table()),
        jnp.asarray(order_table()),
        jnp.asarray(hann_row()),
        band_gain,
        pair_mask,
    )
    stacks = pl.pallas_call(
        place_kernel,
        out_shape=jax.ShapeDtypeStruct((5, BS, BS, 2, NB), F32),
        in_specs=[any_space],
        out_specs=any_space,
        scratch_shapes=[pltpu.VMEM((5, BS, 2, BS, NB), F32), dma((5,)), dma((5, 2))],
        cost_estimate=pl.CostEstimate(flops=0, bytes_accessed=8 * 10**6, transcendentals=0),
    )(sums)
    return stacks[None]


def solution(mesh):
    placed = (P("tm", None, "chan", None, None), P(), P(("tm", "chan"), None))
    return jax.shard_map(
        body,
        mesh=mesh,
        in_specs=placed,
        out_specs=P(("tm", "chan"), None, None, None, None, None),
        check_vma=False,
    )
```

```python
import jax
import jax.numpy as jnp
import ml_dtypes
import numpy as np
from jax import lax
from jax.experimental import pallas as pl
from jax.experimental.pallas import tpu as pltpu
from jax.sharding import PartitionSpec as P

L = 4096
F0 = 8
HW = 64
NB = 384
EXT = NB + 2 * HW
NTM = 16
NCHAN = 8
NBLK = NTM * NCHAN
BS = 16
WL = 4
ROWS = NTM * BS
MESH = pl.DeviceIdType.MESH
F32 = jnp.float32
BF16 = jnp.bfloat16
OWN, ABOVE, X1, X2, BELOW = range(5)


def bin_order():
    j = np.arange(EXT)
    return np.concatenate([j[j % 4 == 0], j[j % 4 == 2], j[j % 2 == 1]])


def dft_tables():
    order = bin_order()

    def parts(samples, bins):
        phase = (np.arange(samples)[:, None] * (F0 + bins)[None, :] % L) * (2 * np.pi / L)
        return np.cos(phase) / 64.0, -np.sin(phase) / 64.0

    quarter = EXT // 4
    even = []
    for r in range(2):
        even += parts(L // 4, order[r * quarter : (r + 1) * quarter])
    even = np.concatenate(even, axis=1)
    odd = np.concatenate(parts(L // 2, order[2 * quarter :]), axis=1)

    def split(table):
        high = table.astype(ml_dtypes.bfloat16)
        low = (table - high.astype(np.float64)).astype(ml_dtypes.bfloat16)
        return np.stack([high, low])

    return np.concatenate([split(even), split(odd)], axis=1)


def smoother_table():
    order = bin_order()
    lower = order - HW
    covered = (order[:, None] >= lower[None, :]) & (order[:, None] <= lower[None, :] + 2 * HW)
    return covered.astype(ml_dtypes.bfloat16)


def order_table():
    order = bin_order()
    return (order[:, None] == np.arange(NB)[None, :] + HW).astype(ml_dtypes.bfloat16)


def hann_row():
    n = np.arange(L)
    return (0.5 - 0.5 * np.cos(2 * np.pi * n / L)).astype(np.float32)[None, :]


def device_of(block):
    wrapped = lax.rem(block + NBLK, NBLK)
    return (wrapped // NCHAN, lax.rem(wrapped, NCHAN))


def kernel(
    rec,
    tab_hbm,
    smooth,
    perm,
    hann,
    gain,
    mask,
    out,
    xbuf,
    tab,
    fold,
    spec,
    pw,
    lev,
    wh,
    gperm,
    send,
    blocks,
    wide,
    other,
    acc,
    give,
    take,
    rec_sem,
    tab_sem,
    a2a_s,
    a2a_r,
    dup_s,
    dup_r,
    ring_s,
    ring_r,
    sib_s,
    sib_r,
    give_s,
    give_r,
    out_sem,
):
    t = lax.axis_index("tm")
    c = lax.axis_index("chan")
    block = t * NCHAN + c
    core = lax.rem(c, 2)
    before = device_of(block - 2)
    after = device_of(block + 2)
    sibling = (t, c + 1 - 2 * core)
    first = c < 2
    last = c >= NCHAN - 2
    shift = jnp.where(first, 1, -1)
    round_corner = lax.rem(c + 6 * shift + NCHAN, NCHAN)
    dup_slot = jnp.where(first, ABOVE, BELOW)

    def rec_copy(w):
        slot = lax.rem(w, 2)
        return pltpu.make_async_copy(rec.at[w], xbuf.at[slot], rec_sem.at[slot])

    tab_copy = pltpu.make_async_copy(tab_hbm, tab, tab_sem)
    rec_copy(0).start()
    tab_copy.start()
    rec_copy(1).start()

    barrier = pltpu.get_barrier_semaphore()
    for d in range(1, NTM):
        pl.semaphore_signal(
            barrier, inc=1, device_id=(lax.rem(t + d, NTM), c), device_id_type=MESH
        )
    pl.semaphore_signal(barrier, inc=1, device_id=sibling, device_id_type=MESH)

    @pl.when(jnp.logical_not(first))
    def _():
        pl.semaphore_signal(barrier, inc=1, device_id=before, device_id_type=MESH)

    @pl.when(jnp.logical_not(last))
    def _():
        pl.semaphore_signal(barrier, inc=1, device_id=after, device_id_type=MESH)

    @pl.when(first | last)
    def _():
        for d in range(NTM):
            pl.semaphore_signal(
                barrier, inc=1, device_id=(lax.rem(t + d, NTM), round_corner), device_id_type=MESH
            )

    def clear(i, _):
        acc[i // 16, lax.rem(i, 16)] = jnp.zeros((2, BS, NB), F32)
        return 0

    lax.fori_loop(0, 80, clear, 0)

    rest = jnp.broadcast_to(gain[...].reshape(1, NB), (16, NB))
    total = jnp.zeros((16, EXT), F32)
    for _ in range(3):
        piece = rest.astype(BF16)
        rest = rest - piece.astype(F32)
        total += lax.dot_general(
            piece, perm[...], (((1,), (1,)), ((), ())), preferred_element_type=F32
        )
    gperm[...] = total

    def a2a_copy(w, d):
        q = lax.rem(t + d, NTM)
        return pltpu.make_async_remote_copy(
            src_ref=send.at[w, pl.ds(pl.multiple_of(q * BS, BS), BS)],
            dst_ref=blocks.at[OWN, w, t],
            send_sem=a2a_s.at[w, d],
            recv_sem=a2a_r.at[w, d],
            device_id=(q, c),
            device_id_type=MESH,
        )

    def dup_copy(w, d):
        r = lax.rem(t + d, NTM)
        q = lax.rem(r + shift + NTM, NTM)
        return pltpu.make_async_remote_copy(
            src_ref=send.at[w, pl.ds(pl.multiple_of(q * BS, BS), BS)],
            dst_ref=blocks.at[dup_slot, w, t],
            send_sem=dup_s.at[w, d],
            recv_sem=dup_r.at[w, d],
            device_id=(r, round_corner),
            device_id_type=MESH,
        )

    def bins_of(ref, slot, w, f):
        return ref.at[slot, w, :, :, pl.ds(pl.multiple_of(f * 256, 256), 256)]

    def ring_copy(w, up, f):
        return pltpu.make_async_remote_copy(
            src_ref=bins_of(blocks, OWN, w, f),
            dst_ref=bins_of(blocks, ABOVE if up else BELOW, w, f),
            send_sem=ring_s.at[w, f, up],
            recv_sem=ring_r.at[w, f, up],
            device_id=before if up else after,
            device_id_type=MESH,
        )

    def sib_copy(w, source, slot, f):
        return pltpu.make_async_remote_copy(
            src_ref=bins_of(blocks, source, w, f),
            dst_ref=bins_of(blocks, slot, w, f),
            send_sem=sib_s.at[w, f, slot - X1],
            recv_sem=sib_r.at[w, f, slot - X1],
            device_id=sibling,
            device_id_type=MESH,
        )

    def widen(which, source, w, f):
        at = pl.ds(pl.multiple_of(f * 256, 256), 256)
        to = pl.multiple_of(f * 384, 384)

        def one(i, _):
            both = blocks[source, w, i, :, at].astype(F32)
            wide[which, w, i, :, pl.ds(to, 256)] = both
            wide[which, w, i, :, pl.ds(to + 256, 128)] = both[:, :128] + both[:, 128:]
            return 0

        lax.fori_loop(0, NTM, one, 0, unroll=4)

    def widen_other(slot, w, f):
        at = pl.ds(pl.multiple_of(f * 256, 256), 256)

        def one(i, _):
            other[slot - ABOVE, i] = blocks[slot, w, i, :, at].astype(F32)
            return 0

        lax.fori_loop(0, NTM, one, 0, unroll=4)

    def spread(w):
        for d in range(1, NTM):
            a2a_copy(w, d).wait_recv()
        for f in range(3):

            @pl.when(jnp.logical_not(first))
            def _():
                ring_copy(w, 1, f).start()

            @pl.when(jnp.logical_not(last))
            def _():
                ring_copy(w, 0, f).start()

            @pl.when(core == 1)
            def _():
                sib_copy(w, OWN, X1, f).start()

        for f in range(3):
            widen(0, OWN, w, f)

    def transform(w, _):
        slot = lax.rem(w, 2)
        rec_copy(w).wait()

        def fold_rows(i, _):
            rows = pl.ds(pl.multiple_of(i * 16, 16), 16)
            low_rows = pl.ds(pl.multiple_of(ROWS + i * 16, 16), 16)

            def put(value, at):
                high = value.astype(BF16)
                fold[rows, at : at + 128] = high
                fold[low_rows, at : at + 128] = (value - high.astype(F32)).astype(BF16)

            for p in range(0, L // 4, 128):
                x0, x1, x2, x3 = (
                    xbuf[slot, rows, s + p : s + p + 128] * hann[:, s + p : s + p + 128]
                    for s in range(0, L, L // 4)
                )
                u, v = x0 + x2, x1 + x3
                put(u + v, p)
                put(u - v, L // 4 + p)
                put(x0 - x2, L // 2 + p)
                put(x1 - x3, 3 * L // 4 + p)
            return 0

        lax.fori_loop(0, ROWS // 16, fold_rows, 0)

        @pl.when(w + 2 < WL)
        def _():
            rec_copy(w + 2).start()

        @pl.when(w == 0)
        def _():
            tab_copy.wait()

        def product(at, length, trow, tcol, col):
            both = jnp.dot(
                fold[:, at : at + length],
                tab[0, trow : trow + length, tcol : tcol + 256],
                preferred_element_type=F32,
            )
            low = jnp.dot(
                fold[:ROWS, at : at + length],
                tab[1, trow : trow + length, tcol : tcol + 256],
                preferred_element_type=F32,
            )
            spec[:, col : col + 256] = both[:ROWS] + (both[ROWS:] + low)

        product(0, L // 4, 0, 0, 0)
        product(L // 4, L // 4, 0, 256, 256)
        product(L // 2, L // 2, L // 4, 0, 512)
        product(L // 2, L // 2, L // 4, 256, 768)

        def spectrum(rows):
            re = jnp.concatenate([spec[rows, 0:128], spec[rows, 256:384], spec[rows, 512:768]], 1)
            im = jnp.concatenate([spec[rows, 128:256], spec[rows, 384:512], spec[rows, 768:1024]], 1)
            return re, im

        def power_rows(i, _):
            rows = pl.ds(pl.multiple_of(i * 16, 16), 16)
            re, im = spectrum(rows)
            power = re * re + im * im
            high = power.astype(BF16)
            pw[rows] = high
            pw[pl.ds(pl.multiple_of(ROWS + i * 16, 16), 16)] = (power - high.astype(F32)).astype(BF16)
            return 0

        lax.fori_loop(0, ROWS // 16, power_rows, 0)
        lev[...] = jnp.dot(pw[...], smooth[...], preferred_element_type=F32)

        def white_rows(i, _):
            rows = pl.ds(pl.multiple_of(i * 16, 16), 16)
            low_rows = pl.ds(pl.multiple_of(ROWS + i * 16, 16), 16)
            level = (lev[rows] + lev[low_rows]) / (2 * HW + 1)
            factor = gperm[...] * lax.rsqrt(level + 1e-6)
            re, im = spectrum(rows)
            wh[rows] = (re * factor).astype(BF16)
            wh[low_rows] = (im * factor).astype(BF16)
            return 0

        lax.fori_loop(0, ROWS // 16, white_rows, 0)
        white = jnp.dot(wh[...], perm[...], preferred_element_type=F32)
        for f in range(3):
            at = f * 256
            send[w, :, at : at + 128] = white[:ROWS, f * 128 : f * 128 + 128].astype(BF16)
            send[w, :, at + 128 : at + 256] = white[ROWS:, f * 128 : f * 128 + 128].astype(BF16)

        @pl.when((w == 0) & jnp.logical_not(first | last))
        def _():
            pl.semaphore_wait(barrier, NTM - 1 + 3)

        @pl.when((w == 0) & (first | last))
        def _():
            pl.semaphore_wait(barrier, NTM - 1 + 2 + NTM)

        for d in range(1, NTM):
            a2a_copy(w, d).start()
        blocks[OWN, w, t] = send[w, pl.ds(pl.multiple_of(t * BS, BS), BS)]

        @pl.when((w > 0) & (first | last))
        def _():
            for d in range(NTM):
                dup_copy(w - 1, d).start()

        @pl.when(w > 0)
        def _():
            spread(w - 1)

        return 0

    lax.fori_loop(0, WL, transform, 0)

    @pl.when(first | last)
    def _():
        for d in range(NTM):
            dup_copy(WL - 1, d).start()

    def correlate(k, left, right, w, f):
        re_at = pl.ds(pl.multiple_of(f * 384, 128), 128)
        im_at = pl.ds(pl.multiple_of(f * 384 + 128, 128), 128)
        sum_at = pl.ds(pl.multiple_of(f * 384 + 256, 128), 128)
        at = pl.ds(pl.multiple_of(f * 128, 128), 128)
        zero = jnp.zeros((BS, 128), F32)
        for part in range(4):
            mine = range(part * 4, part * 4 + 4)

            def window(n, sums):
                if right is None:
                    cr = wide[0, w, n, :, re_at]
                    ci = wide[0, w, n, :, im_at]
                else:
                    cr = other[right, n, :, :128]
                    ci = other[right, n, :, 128:]
                plus, minus = cr + ci, cr - ci
                new = []
                for i, a in enumerate(mine):
                    new.append(sums[3 * i] + wide[left, w, n, a : a + 1, sum_at] * cr)
                    new.append(sums[3 * i + 1] + wide[left, w, n, a : a + 1, re_at] * plus)
                    new.append(sums[3 * i + 2] + wide[left, w, n, a : a + 1, im_at] * minus)
                return tuple(new)

            sums = lax.fori_loop(0, NTM, window, (zero,) * 12, unroll=8)
            for i, a in enumerate(mine):
                acc[k, a, 0, :, at] += sums[3 * i] - sums[3 * i + 2]
                acc[k, a, 1, :, at] += sums[3 * i] - sums[3 * i + 1]

    def selfs(i, _):
        correlate(0, 0, None, i // 3, lax.rem(i, 3))
        return 0

    lax.fori_loop(0, 3 * (WL - 1), selfs, 0)
    spread(WL - 1)
    lax.fori_loop(3 * (WL - 1), 3 * WL, selfs, 0)

    def give_copy(i, f):
        return pltpu.make_async_remote_copy(
            src_ref=give.at[i, f],
            dst_ref=take.at[i, f],
            send_sem=give_s.at[i, f],
            recv_sem=give_r.at[i, f],
            device_id=before,
            device_id_type=MESH,
        )

    def hand_over(i, k, f):
        at = pl.ds(pl.multiple_of(f * 128, 128), 128)

        def one(a, _):
            give[i, f, a] = acc[k, a, :, :, at].astype(BF16)
            return 0

        lax.fori_loop(0, BS, one, 0, unroll=4)
        give_copy(i, f).start()

    left3 = core
    right3 = X2 - core - ABOVE

    def arrive(i):
        w = i // 3
        f = lax.rem(i, 3)

        @pl.when(jnp.logical_not(last))
        def _():
            ring_copy(w, 1, f).wait_recv()

        @pl.when(jnp.logical_not(first))
        def _():
            ring_copy(w, 0, f).wait_recv()

        @pl.when((first | last) & (f == 0))
        def _():
            for d in range(NTM):
                dup_copy(w, d).wait_recv()

        @pl.when(core == 0)
        def _():
            sib_copy(w, ABOVE, X1, f).start()

        @pl.when(core == 1)
        def _():
            sib_copy(w, ABOVE, X2, f).start()

        widen(1, BELOW, w, f)
        widen_other(ABOVE, w, f)
        correlate(4, 1, ABOVE - ABOVE, w, f)

        @pl.when(w == WL - 1)
        def _():
            hand_over(0, 4, f)

        correlate(2, 0, ABOVE - ABOVE, w, f)

    def use_shared(i):
        w = i // 3
        f = lax.rem(i, 3)
        sib_copy(w, OWN, X1, f).wait_recv()
        widen_other(X1, w, f)

        @pl.when(core == 0)
        def _():
            sib_copy(w, OWN, X2, f).wait_recv()
            widen_other(X2, w, f)

        correlate(3, left3, right3, w, f)

        @pl.when((w == WL - 1) & (core == 1))
        def _():
            hand_over(1, 3, f)

        correlate(1, 0, X1 - ABOVE, w, f)

    def partners(i, _):
        @pl.when(i < 3 * WL)
        def _():
            arrive(i)

        @pl.when(i > 0)
        def _():
            use_shared(i - 1)

        return 0

    def out_copy(k, p):
        return pltpu.make_async_copy(acc.at[k, :, p], out.at[k, :, p], out_sem.at[k, p])

    def weight_of(k):
        inside = (block + k < NBLK).astype(F32)
        return mask[0, k].astype(F32) * inside * (1.0 / 64.0)

    def finish(k):
        weight = weight_of(k)

        def one(a, _):
            acc[k, a] = acc[k, a] * weight
            return 0

        lax.fori_loop(0, BS, one, 0, unroll=2)
        for p in range(2):
            out_copy(k, p).start()

    def finish_taken(k, i):
        weight = weight_of(k)
        for f in range(3):
            give_copy(i, f).wait_recv()

            def one(a, _):
                acc[k, a, :, :, f * 128 : f * 128 + 128] = take[i, f, a].astype(F32) * weight
                return 0

            lax.fori_loop(0, BS, one, 0, unroll=4)
        for p in range(2):
            out_copy(k, p).start()

    finish(0)
    lax.fori_loop(0, 3 * WL + 1, partners, 0)

    finish(2)
    finish(1)

    @pl.when(core == 0)
    def _():
        finish(3)

    finish_taken(4, 0)

    @pl.when(core == 1)
    def _():
        finish_taken(3, 1)

    def drain(i, _):
        w = i // 3
        f = lax.rem(i, 3)

        @pl.when(f == 0)
        def _():
            for d in range(1, NTM):
                a2a_copy(w, d).wait_send()

        @pl.when((first | last) & (f == 0))
        def _():
            for d in range(NTM):
                dup_copy(w, d).wait_send()

        @pl.when(jnp.logical_not(first))
        def _():
            ring_copy(w, 1, f).wait_send()

        @pl.when(jnp.logical_not(last))
        def _():
            ring_copy(w, 0, f).wait_send()

        @pl.when(core == 0)
        def _():
            sib_copy(w, ABOVE, X1, f).wait_send()

        @pl.when(core == 1)
        def _():
            sib_copy(w, OWN, X1, f).wait_send()
            sib_copy(w, ABOVE, X2, f).wait_send()

        return 0

    lax.fori_loop(0, 3 * WL, drain, 0)
    for f in range(3):
        give_copy(0, f).wait_send()

        @pl.when(core == 1)
        def _():
            give_copy(1, f).wait_send()

    for k in range(5):
        for p in range(2):
            out_copy(k, p).wait()


def place_kernel(sums, out, held, in_sem, out_sem):
    def take_in(k):
        return pltpu.make_async_copy(sums.at[k], held.at[k], in_sem.at[k])

    def put_out(k, p):
        return pltpu.make_async_copy(held.at[k, :, p], out.at[k, :, :, p], out_sem.at[k, p])

    for k in range(5):
        take_in(k).start()
    for k in range(5):
        take_in(k).wait()
        for p in range(2):
            put_out(k, p).start()
    for k in range(5):
        for p in range(2):
            put_out(k, p).wait()


def body(records, band_gain, pair_mask):
    rec = records.reshape(WL, ROWS, L)
    any_space = pl.BlockSpec(memory_space=pl.ANY)
    vmem = pl.BlockSpec(memory_space=pltpu.VMEM)
    smem = pl.BlockSpec(memory_space=pltpu.SMEM)
    dma = pltpu.SemaphoreType.DMA
    sums = pl.pallas_call(
        kernel,
        out_shape=jax.ShapeDtypeStruct((5, BS, 2, BS, NB), F32),
        in_specs=[any_space, any_space, vmem, vmem, vmem, vmem, smem],
        out_specs=any_space,
        scratch_shapes=[
            pltpu.VMEM((2, ROWS, L), F32),
            pltpu.VMEM((2, 3 * L // 4, 512), BF16),
            pltpu.VMEM((2 * ROWS, L), BF16),
            pltpu.VMEM((ROWS, 2 * EXT), F32),
            pltpu.VMEM((2 * ROWS, EXT), BF16),
            pltpu.VMEM((2 * ROWS, EXT), F32),
            pltpu.VMEM((2 * ROWS, EXT), BF16),
            pltpu.VMEM((16, EXT), F32),
            pltpu.VMEM((WL, ROWS, 2 * NB), BF16),
            pltpu.VMEM((5, WL, NTM, BS, 2 * NB), BF16),
            pltpu.VMEM((2, WL, NTM, BS, 3 * NB), F32),
            pltpu.VMEM((3, NTM, BS, 256), F32),
            pltpu.VMEM((5, BS, 2, BS, NB), F32),
            pltpu.VMEM((2, 3, BS, 2, BS, 128), BF16),
            pltpu.VMEM((2, 3, BS, 2, BS, 128), BF16),
            dma((2,)),
            dma,
            dma((WL, NTM)),
            dma((WL, NTM)),
            dma((WL, NTM)),
            dma((WL, NTM)),
            dma((WL, 3, 2)),
            dma((WL, 3, 2)),
            dma((WL, 3, 2)),
            dma((WL, 3, 2)),
            dma((2, 3)),
            dma((2, 3)),
            dma((5, 2)),
        ],
        compiler_params=pltpu.CompilerParams(
            collective_id=0, has_side_effects=True, vmem_limit_bytes=58 << 20
        ),
        cost_estimate=pl.CostEstimate(
            flops=10**10, bytes_accessed=30 * 10**6, transcendentals=10**6
        ),
    )(
        rec,
        jnp.asarray(dft_tables()),
        jnp.asarray(smoother_table()),
        jnp.asarray(order_table()),
        jnp.asarray(hann_row()),
        band_gain,
        pair_mask,
    )
    stacks = pl.pallas_call(
        place_kernel,
        out_shape=jax.ShapeDtypeStruct((5, BS, BS, 2, NB), F32),
        in_specs=[any_space],
        out_specs=any_space,
        scratch_shapes=[pltpu.VMEM((5, BS, 2, BS, NB), F32), dma((5,)), dma((5, 2))],
        cost_estimate=pl.CostEstimate(flops=0, bytes_accessed=8 * 10**6, transcendentals=0),
    )(sums)
    return stacks[None]


def solution(mesh):
    placed = (P("tm", None, "chan", None, None), P(), P(("tm", "chan"), None))
    return jax.shard_map(
        body,
        mesh=mesh,
        in_specs=placed,
        out_specs=P(("tm", "chan"), None, None, None, None, None),
        check_vma=False,
    )
```

```python
import jax
import jax.numpy as jnp
import ml_dtypes
import numpy as np
from jax import lax
from jax.experimental import pallas as pl
from jax.experimental.pallas import tpu as pltpu
from jax.sharding import PartitionSpec as P

L = 4096
F0 = 8
HW = 64
NB = 384
EXT = NB + 2 * HW
NTM = 16
NCHAN = 8
NBLK = NTM * NCHAN
BS = 16
WL = 4
ROWS = NTM * BS
MESH = pl.DeviceIdType.MESH
F32 = jnp.float32
BF16 = jnp.bfloat16
OWN, ABOVE, X1, X2, BELOW = range(5)


def bin_order():
    j = np.arange(EXT)
    return np.concatenate([j[j % 4 == 0], j[j % 4 == 2], j[j % 2 == 1]])


def dft_tables():
    order = bin_order()

    def parts(samples, bins):
        phase = (np.arange(samples)[:, None] * (F0 + bins)[None, :] % L) * (2 * np.pi / L)
        return np.cos(phase) / 64.0, -np.sin(phase) / 64.0

    quarter = EXT // 4
    even = []
    for r in range(2):
        even += parts(L // 4, order[r * quarter : (r + 1) * quarter])
    even = np.concatenate(even, axis=1)
    odd = np.concatenate(parts(L // 2, order[2 * quarter :]), axis=1)

    def split(table):
        high = table.astype(ml_dtypes.bfloat16)
        low = (table - high.astype(np.float64)).astype(ml_dtypes.bfloat16)
        return np.stack([high, low])

    return np.concatenate([split(even), split(odd)], axis=1)


def smoother_table():
    order = bin_order()
    lower = order - HW
    covered = (order[:, None] >= lower[None, :]) & (order[:, None] <= lower[None, :] + 2 * HW)
    return covered.astype(ml_dtypes.bfloat16)


def order_table():
    order = bin_order()
    return (order[:, None] == np.arange(NB)[None, :] + HW).astype(ml_dtypes.bfloat16)


def hann_row():
    n = np.arange(L)
    return (0.5 - 0.5 * np.cos(2 * np.pi * n / L)).astype(np.float32)[None, :]


def device_of(block):
    wrapped = lax.rem(block + NBLK, NBLK)
    return (wrapped // NCHAN, lax.rem(wrapped, NCHAN))


def kernel(
    rec,
    tab_hbm,
    smooth,
    perm,
    hann,
    gain,
    mask,
    out,
    xbuf,
    tab,
    fold,
    spec,
    pw,
    lev,
    wh,
    gperm,
    send,
    blocks,
    wide,
    other,
    acc,
    give,
    take,
    rec_sem,
    tab_sem,
    a2a_s,
    a2a_r,
    dup_s,
    dup_r,
    ring_s,
    ring_r,
    sib_s,
    sib_r,
    give_s,
    give_r,
    out_sem,
):
    t = lax.axis_index("tm")
    c = lax.axis_index("chan")
    block = t * NCHAN + c
    core = lax.rem(c, 2)
    before = device_of(block - 2)
    after = device_of(block + 2)
    sibling = (t, c + 1 - 2 * core)
    first = c < 2
    last = c >= NCHAN - 2
    shift = jnp.where(first, 1, -1)
    round_corner = lax.rem(c + 6 * shift + NCHAN, NCHAN)
    dup_slot = jnp.where(first, ABOVE, BELOW)

    def rec_copy(w):
        slot = lax.rem(w, 2)
        return pltpu.make_async_copy(rec.at[w], xbuf.at[slot], rec_sem.at[slot])

    tab_copy = pltpu.make_async_copy(tab_hbm, tab, tab_sem)
    rec_copy(0).start()
    tab_copy.start()
    rec_copy(1).start()

    barrier = pltpu.get_barrier_semaphore()
    for d in range(1, NTM):
        pl.semaphore_signal(
            barrier, inc=1, device_id=(lax.rem(t + d, NTM), c), device_id_type=MESH
        )
    pl.semaphore_signal(barrier, inc=1, device_id=sibling, device_id_type=MESH)

    @pl.when(jnp.logical_not(first))
    def _():
        pl.semaphore_signal(barrier, inc=1, device_id=before, device_id_type=MESH)

    @pl.when(jnp.logical_not(last))
    def _():
        pl.semaphore_signal(barrier, inc=1, device_id=after, device_id_type=MESH)

    @pl.when(first | last)
    def _():
        for d in range(NTM):
            pl.semaphore_signal(
                barrier, inc=1, device_id=(lax.rem(t + d, NTM), round_corner), device_id_type=MESH
            )

    def clear(i, _):
        acc[i // 16, lax.rem(i, 16)] = jnp.zeros((2, BS, NB), F32)
        return 0

    lax.fori_loop(0, 80, clear, 0)

    rest = jnp.broadcast_to(gain[...].reshape(1, NB), (16, NB))
    total = jnp.zeros((16, EXT), F32)
    for _ in range(3):
        piece = rest.astype(BF16)
        rest = rest - piece.astype(F32)
        total += lax.dot_general(
            piece, perm[...], (((1,), (1,)), ((), ())), preferred_element_type=F32
        )
    gperm[...] = total

    def a2a_copy(w, d):
        q = lax.rem(t + d, NTM)
        return pltpu.make_async_remote_copy(
            src_ref=send.at[w, pl.ds(pl.multiple_of(q * BS, BS), BS)],
            dst_ref=blocks.at[OWN, w, t],
            send_sem=a2a_s.at[w, d],
            recv_sem=a2a_r.at[w, d],
            device_id=(q, c),
            device_id_type=MESH,
        )

    def dup_copy(w, d):
        r = lax.rem(t + d, NTM)
        q = lax.rem(r + shift + NTM, NTM)
        return pltpu.make_async_remote_copy(
            src_ref=send.at[w, pl.ds(pl.multiple_of(q * BS, BS), BS)],
            dst_ref=blocks.at[dup_slot, w, t],
            send_sem=dup_s.at[w, d],
            recv_sem=dup_r.at[w, d],
            device_id=(r, round_corner),
            device_id_type=MESH,
        )

    def bins_of(ref, slot, w, f):
        return ref.at[slot, w, :, :, pl.ds(pl.multiple_of(f * 256, 256), 256)]

    def ring_copy(w, up, f):
        return pltpu.make_async_remote_copy(
            src_ref=bins_of(blocks, OWN, w, f),
            dst_ref=bins_of(blocks, ABOVE if up else BELOW, w, f),
            send_sem=ring_s.at[w, f, up],
            recv_sem=ring_r.at[w, f, up],
            device_id=before if up else after,
            device_id_type=MESH,
        )

    def sib_copy(w, source, slot, f):
        return pltpu.make_async_remote_copy(
            src_ref=bins_of(blocks, source, w, f),
            dst_ref=bins_of(blocks, slot, w, f),
            send_sem=sib_s.at[w, f, slot - X1],
            recv_sem=sib_r.at[w, f, slot - X1],
            device_id=sibling,
            device_id_type=MESH,
        )

    def widen(which, source, w, f):
        at = pl.ds(pl.multiple_of(f * 256, 256), 256)
        to = pl.multiple_of(f * 384, 384)

        def one(i, _):
            both = blocks[source, w, i, :, at].astype(F32)
            wide[which, w, i, :, pl.ds(to, 256)] = both
            wide[which, w, i, :, pl.ds(to + 256, 128)] = both[:, :128] + both[:, 128:]
            return 0

        lax.fori_loop(0, NTM, one, 0, unroll=4)

    def widen_other(slot, w, f):
        at = pl.ds(pl.multiple_of(f * 256, 256), 256)

        def one(i, _):
            other[slot - ABOVE, i] = blocks[slot, w, i, :, at].astype(F32)
            return 0

        lax.fori_loop(0, NTM, one, 0, unroll=4)

    def spread(w):
        for d in range(1, NTM):
            a2a_copy(w, d).wait_recv()
        for f in range(3):

            @pl.when(jnp.logical_not(first))
            def _():
                ring_copy(w, 1, f).start()

            @pl.when(jnp.logical_not(last))
            def _():
                ring_copy(w, 0, f).start()

            @pl.when(core == 1)
            def _():
                sib_copy(w, OWN, X1, f).start()

        for f in range(3):
            widen(0, OWN, w, f)

    def transform(w, _):
        slot = lax.rem(w, 2)
        rec_copy(w).wait()

        def fold_rows(i, _):
            rows = pl.ds(pl.multiple_of(i * 16, 16), 16)
            low_rows = pl.ds(pl.multiple_of(ROWS + i * 16, 16), 16)

            def put(value, at):
                high = value.astype(BF16)
                fold[rows, at : at + 128] = high
                fold[low_rows, at : at + 128] = (value - high.astype(F32)).astype(BF16)

            for p in range(0, L // 4, 128):
                x0, x1, x2, x3 = (
                    xbuf[slot, rows, s + p : s + p + 128] * hann[:, s + p : s + p + 128]
                    for s in range(0, L, L // 4)
                )
                u, v = x0 + x2, x1 + x3
                put(u + v, p)
                put(u - v, L // 4 + p)
                put(x0 - x2, L // 2 + p)
                put(x1 - x3, 3 * L // 4 + p)
            return 0

        lax.fori_loop(0, ROWS // 16, fold_rows, 0)

        @pl.when(w + 2 < WL)
        def _():
            rec_copy(w + 2).start()

        @pl.when(w == 0)
        def _():
            tab_copy.wait()

        def product(at, length, trow, tcol, col):
            both = jnp.dot(
                fold[:, at : at + length],
                tab[0, trow : trow + length, tcol : tcol + 256],
                preferred_element_type=F32,
            )
            low = jnp.dot(
                fold[:ROWS, at : at + length],
                tab[1, trow : trow + length, tcol : tcol + 256],
                preferred_element_type=F32,
            )
            spec[:, col : col + 256] = both[:ROWS] + (both[ROWS:] + low)

        product(0, L // 4, 0, 0, 0)
        product(L // 4, L // 4, 0, 256, 256)
        product(L // 2, L // 2, L // 4, 0, 512)
        product(L // 2, L // 2, L // 4, 256, 768)

        def spectrum(rows):
            re = jnp.concatenate([spec[rows, 0:128], spec[rows, 256:384], spec[rows, 512:768]], 1)
            im = jnp.concatenate([spec[rows, 128:256], spec[rows, 384:512], spec[rows, 768:1024]], 1)
            return re, im

        def power_rows(i, _):
            rows = pl.ds(pl.multiple_of(i * 16, 16), 16)
            re, im = spectrum(rows)
            power = re * re + im * im
            high = power.astype(BF16)
            pw[rows] = high
            pw[pl.ds(pl.multiple_of(ROWS + i * 16, 16), 16)] = (power - high.astype(F32)).astype(BF16)
            return 0

        lax.fori_loop(0, ROWS // 16, power_rows, 0)
        lev[...] = jnp.dot(pw[...], smooth[...], preferred_element_type=F32)

        def white_rows(i, _):
            rows = pl.ds(pl.multiple_of(i * 16, 16), 16)
            low_rows = pl.ds(pl.multiple_of(ROWS + i * 16, 16), 16)
            level = (lev[rows] + lev[low_rows]) / (2 * HW + 1)
            factor = gperm[...] * lax.rsqrt(level + 1e-6)
            re, im = spectrum(rows)
            wh[rows] = (re * factor).astype(BF16)
            wh[low_rows] = (im * factor).astype(BF16)
            return 0

        lax.fori_loop(0, ROWS // 16, white_rows, 0)
        white = jnp.dot(wh[...], perm[...], preferred_element_type=F32)
        for f in range(3):
            at = f * 256
            send[w, :, at : at + 128] = white[:ROWS, f * 128 : f * 128 + 128].astype(BF16)
            send[w, :, at + 128 : at + 256] = white[ROWS:, f * 128 : f * 128 + 128].astype(BF16)

        @pl.when((w == 0) & jnp.logical_not(first | last))
        def _():
            pl.semaphore_wait(barrier, NTM - 1 + 3)

        @pl.when((w == 0) & (first | last))
        def _():
            pl.semaphore_wait(barrier, NTM - 1 + 2 + NTM)

        for d in range(1, NTM):
            a2a_copy(w, d).start()
        blocks[OWN, w, t] = send[w, pl.ds(pl.multiple_of(t * BS, BS), BS)]

        @pl.when((w > 0) & (first | last))
        def _():
            for d in range(NTM):
                dup_copy(w - 1, d).start()

        @pl.when(w > 0)
        def _():
            spread(w - 1)

        return 0

    lax.fori_loop(0, WL, transform, 0)

    @pl.when(first | last)
    def _():
        for d in range(NTM):
            dup_copy(WL - 1, d).start()

    def correlate(k, left, right, w, f):
        re_at = pl.ds(pl.multiple_of(f * 384, 128), 128)
        im_at = pl.ds(pl.multiple_of(f * 384 + 128, 128), 128)
        sum_at = pl.ds(pl.multiple_of(f * 384 + 256, 128), 128)
        at = pl.ds(pl.multiple_of(f * 128, 128), 128)
        zero = jnp.zeros((BS, 128), F32)
        for part in range(4):
            mine = range(part * 4, part * 4 + 4)

            def window(n, sums):
                if right is None:
                    cr = wide[0, w, n, :, re_at]
                    ci = wide[0, w, n, :, im_at]
                else:
                    cr = other[right, n, :, :128]
                    ci = other[right, n, :, 128:]
                plus, minus = cr + ci, cr - ci
                new = []
                for i, a in enumerate(mine):
                    new.append(sums[3 * i] + wide[left, w, n, a : a + 1, sum_at] * cr)
                    new.append(sums[3 * i + 1] + wide[left, w, n, a : a + 1, re_at] * plus)
                    new.append(sums[3 * i + 2] + wide[left, w, n, a : a + 1, im_at] * minus)
                return tuple(new)

            sums = lax.fori_loop(0, NTM, window, (zero,) * 12, unroll=8)
            for i, a in enumerate(mine):
                acc[k, a, 0, :, at] += sums[3 * i] - sums[3 * i + 2]
                acc[k, a, 1, :, at] += sums[3 * i] - sums[3 * i + 1]

    def selfs(i, _):
        correlate(0, 0, None, i // 3, lax.rem(i, 3))
        return 0

    lax.fori_loop(0, 5, selfs, 0)
    spread(WL - 1)
    lax.fori_loop(5, 3 * WL, selfs, 0)

    def give_copy(i, f):
        return pltpu.make_async_remote_copy(
            src_ref=give.at[i, f],
            dst_ref=take.at[i, f],
            send_sem=give_s.at[i, f],
            recv_sem=give_r.at[i, f],
            device_id=before,
            device_id_type=MESH,
        )

    def hand_over(i, k, f):
        at = pl.ds(pl.multiple_of(f * 128, 128), 128)

        def one(a, _):
            give[i, f, a] = acc[k, a, :, :, at].astype(BF16)
            return 0

        lax.fori_loop(0, BS, one, 0, unroll=4)
        give_copy(i, f).start()

    left3 = core
    right3 = X2 - core - ABOVE

    def arrive(i):
        w = i // 3
        f = lax.rem(i, 3)

        @pl.when(jnp.logical_not(last))
        def _():
            ring_copy(w, 1, f).wait_recv()

        @pl.when(jnp.logical_not(first))
        def _():
            ring_copy(w, 0, f).wait_recv()

        @pl.when((first | last) & (f == 0))
        def _():
            for d in range(NTM):
                dup_copy(w, d).wait_recv()

        @pl.when(core == 0)
        def _():
            sib_copy(w, ABOVE, X1, f).start()

        @pl.when(core == 1)
        def _():
            sib_copy(w, ABOVE, X2, f).start()

        widen(1, BELOW, w, f)
        widen_other(ABOVE, w, f)
        correlate(4, 1, ABOVE - ABOVE, w, f)

        @pl.when(w == WL - 1)
        def _():
            hand_over(0, 4, f)

        correlate(2, 0, ABOVE - ABOVE, w, f)

    def use_shared(i):
        w = i // 3
        f = lax.rem(i, 3)
        sib_copy(w, OWN, X1, f).wait_recv()
        widen_other(X1, w, f)

        @pl.when(core == 0)
        def _():
            sib_copy(w, OWN, X2, f).wait_recv()
            widen_other(X2, w, f)

        correlate(3, left3, right3, w, f)

        @pl.when((w == WL - 1) & (core == 1))
        def _():
            hand_over(1, 3, f)

        correlate(1, 0, X1 - ABOVE, w, f)

    def partners(i, _):
        @pl.when(i < 3 * WL)
        def _():
            arrive(i)

        @pl.when(i > 0)
        def _():
            use_shared(i - 1)

        return 0

    def out_copy(k, p):
        return pltpu.make_async_copy(acc.at[k, :, p], out.at[k, :, p], out_sem.at[k, p])

    def weight_of(k):
        inside = (block + k < NBLK).astype(F32)
        return mask[0, k].astype(F32) * inside * (1.0 / 64.0)

    def finish(k):
        weight = weight_of(k)

        def one(a, _):
            acc[k, a] = acc[k, a] * weight
            return 0

        lax.fori_loop(0, BS, one, 0, unroll=2)
        for p in range(2):
            out_copy(k, p).start()

    def finish_taken(k, i):
        weight = weight_of(k)
        for f in range(3):
            give_copy(i, f).wait_recv()

            def one(a, _):
                acc[k, a, :, :, f * 128 : f * 128 + 128] = take[i, f, a].astype(F32) * weight
                return 0

            lax.fori_loop(0, BS, one, 0, unroll=4)
        for p in range(2):
            out_copy(k, p).start()

    finish(0)
    lax.fori_loop(0, 3 * WL + 1, partners, 0)

    finish(2)
    finish(1)

    @pl.when(core == 0)
    def _():
        finish(3)

    finish_taken(4, 0)

    @pl.when(core == 1)
    def _():
        finish_taken(3, 1)

    def drain(i, _):
        w = i // 3
        f = lax.rem(i, 3)

        @pl.when(f == 0)
        def _():
            for d in range(1, NTM):
                a2a_copy(w, d).wait_send()

        @pl.when((first | last) & (f == 0))
        def _():
            for d in range(NTM):
                dup_copy(w, d).wait_send()

        @pl.when(jnp.logical_not(first))
        def _():
            ring_copy(w, 1, f).wait_send()

        @pl.when(jnp.logical_not(last))
        def _():
            ring_copy(w, 0, f).wait_send()

        @pl.when(core == 0)
        def _():
            sib_copy(w, ABOVE, X1, f).wait_send()

        @pl.when(core == 1)
        def _():
            sib_copy(w, OWN, X1, f).wait_send()
            sib_copy(w, ABOVE, X2, f).wait_send()

        return 0

    lax.fori_loop(0, 3 * WL, drain, 0)
    for f in range(3):
        give_copy(0, f).wait_send()

        @pl.when(core == 1)
        def _():
            give_copy(1, f).wait_send()

    for k in range(5):
        for p in range(2):
            out_copy(k, p).wait()


def place_kernel(sums, out, held, in_sem, out_sem):
    def take_in(k):
        return pltpu.make_async_copy(sums.at[k], held.at[k], in_sem.at[k])

    def put_out(k, p):
        return pltpu.make_async_copy(held.at[k, :, p], out.at[k, :, :, p], out_sem.at[k, p])

    for k in range(5):
        take_in(k).start()
    for k in range(5):
        take_in(k).wait()
        for p in range(2):
            put_out(k, p).start()
    for k in range(5):
        for p in range(2):
            put_out(k, p).wait()


def body(records, band_gain, pair_mask):
    rec = records.reshape(WL, ROWS, L)
    any_space = pl.BlockSpec(memory_space=pl.ANY)
    vmem = pl.BlockSpec(memory_space=pltpu.VMEM)
    smem = pl.BlockSpec(memory_space=pltpu.SMEM)
    dma = pltpu.SemaphoreType.DMA
    sums = pl.pallas_call(
        kernel,
        out_shape=jax.ShapeDtypeStruct((5, BS, 2, BS, NB), F32),
        in_specs=[any_space, any_space, vmem, vmem, vmem, vmem, smem],
        out_specs=any_space,
        scratch_shapes=[
            pltpu.VMEM((2, ROWS, L), F32),
            pltpu.VMEM((2, 3 * L // 4, 512), BF16),
            pltpu.VMEM((2 * ROWS, L), BF16),
            pltpu.VMEM((ROWS, 2 * EXT), F32),
            pltpu.VMEM((2 * ROWS, EXT), BF16),
            pltpu.VMEM((2 * ROWS, EXT), F32),
            pltpu.VMEM((2 * ROWS, EXT), BF16),
            pltpu.VMEM((16, EXT), F32),
            pltpu.VMEM((WL, ROWS, 2 * NB), BF16),
            pltpu.VMEM((5, WL, NTM, BS, 2 * NB), BF16),
            pltpu.VMEM((2, WL, NTM, BS, 3 * NB), F32),
            pltpu.VMEM((3, NTM, BS, 256), F32),
            pltpu.VMEM((5, BS, 2, BS, NB), F32),
            pltpu.VMEM((2, 3, BS, 2, BS, 128), BF16),
            pltpu.VMEM((2, 3, BS, 2, BS, 128), BF16),
            dma((2,)),
            dma,
            dma((WL, NTM)),
            dma((WL, NTM)),
            dma((WL, NTM)),
            dma((WL, NTM)),
            dma((WL, 3, 2)),
            dma((WL, 3, 2)),
            dma((WL, 3, 2)),
            dma((WL, 3, 2)),
            dma((2, 3)),
            dma((2, 3)),
            dma((5, 2)),
        ],
        compiler_params=pltpu.CompilerParams(
            collective_id=0, has_side_effects=True, vmem_limit_bytes=58 << 20
        ),
        cost_estimate=pl.CostEstimate(
            flops=10**10, bytes_accessed=30 * 10**6, transcendentals=10**6
        ),
    )(
        rec,
        jnp.asarray(dft_tables()),
        jnp.asarray(smoother_table()),
        jnp.asarray(order_table()),
        jnp.asarray(hann_row()),
        band_gain,
        pair_mask,
    )
    stacks = pl.pallas_call(
        place_kernel,
        out_shape=jax.ShapeDtypeStruct((5, BS, BS, 2, NB), F32),
        in_specs=[any_space],
        out_specs=any_space,
        scratch_shapes=[pltpu.VMEM((5, BS, 2, BS, NB), F32), dma((5,)), dma((5, 2))],
        cost_estimate=pl.CostEstimate(flops=0, bytes_accessed=8 * 10**6, transcendentals=0),
    )(sums)
    return stacks[None]


def solution(mesh):
    placed = (P("tm", None, "chan", None, None), P(), P(("tm", "chan"), None))
    return jax.shard_map(
        body,
        mesh=mesh,
        in_specs=placed,
        out_specs=P(("tm", "chan"), None, None, None, None, None),
        check_vma=False,
    )
```

```python
import jax
import jax.numpy as jnp
import ml_dtypes
import numpy as np
from jax import lax
from jax.experimental import pallas as pl
from jax.experimental.pallas import tpu as pltpu
from jax.sharding import PartitionSpec as P

L = 4096
F0 = 8
HW = 64
NB = 384
EXT = NB + 2 * HW
NTM = 16
NCHAN = 8
NBLK = NTM * NCHAN
BS = 16
WL = 4
ROWS = NTM * BS
MESH = pl.DeviceIdType.MESH
F32 = jnp.float32
BF16 = jnp.bfloat16
OWN, ABOVE, X1, X2, BELOW = range(5)


def bin_order():
    j = np.arange(EXT)
    return np.concatenate([j[j % 4 == 0], j[j % 4 == 2], j[j % 2 == 1]])


def dft_tables():
    order = bin_order()

    def parts(samples, bins):
        phase = (np.arange(samples)[:, None] * (F0 + bins)[None, :] % L) * (2 * np.pi / L)
        return np.cos(phase) / 64.0, -np.sin(phase) / 64.0

    quarter = EXT // 4
    even = []
    for r in range(2):
        even += parts(L // 4, order[r * quarter : (r + 1) * quarter])
    even = np.concatenate(even, axis=1)
    odd = np.concatenate(parts(L // 2, order[2 * quarter :]), axis=1)

    def split(table):
        high = table.astype(ml_dtypes.bfloat16)
        low = (table - high.astype(np.float64)).astype(ml_dtypes.bfloat16)
        return np.stack([high, low])

    return np.concatenate([split(even), split(odd)], axis=1)


def smoother_table():
    order = bin_order()
    lower = order - HW
    covered = (order[:, None] >= lower[None, :]) & (order[:, None] <= lower[None, :] + 2 * HW)
    return covered.astype(ml_dtypes.bfloat16)


def order_table():
    order = bin_order()
    return (order[:, None] == np.arange(NB)[None, :] + HW).astype(ml_dtypes.bfloat16)


def hann_row():
    n = np.arange(L)
    return (0.5 - 0.5 * np.cos(2 * np.pi * n / L)).astype(np.float32)[None, :]


def device_of(block):
    wrapped = lax.rem(block + NBLK, NBLK)
    return (wrapped // NCHAN, lax.rem(wrapped, NCHAN))


def kernel(
    rec,
    tab_hbm,
    smooth,
    perm,
    hann,
    gain,
    mask,
    out,
    xbuf,
    tab,
    fold,
    spec,
    pw,
    lev,
    wh,
    gperm,
    send,
    blocks,
    wide,
    other,
    acc,
    give,
    take,
    rec_sem,
    tab_sem,
    a2a_s,
    a2a_r,
    dup_s,
    dup_r,
    ring_s,
    ring_r,
    sib_s,
    sib_r,
    give_s,
    give_r,
    out_sem,
):
    t = lax.axis_index("tm")
    c = lax.axis_index("chan")
    block = t * NCHAN + c
    core = lax.rem(c, 2)
    before = device_of(block - 2)
    after = device_of(block + 2)
    sibling = (t, c + 1 - 2 * core)
    first = c < 2
    last = c >= NCHAN - 2
    shift = jnp.where(first, 1, -1)
    round_corner = lax.rem(c + 6 * shift + NCHAN, NCHAN)
    dup_slot = jnp.where(first, ABOVE, BELOW)

    def rec_copy(w):
        slot = lax.rem(w, 2)
        return pltpu.make_async_copy(rec.at[w], xbuf.at[slot], rec_sem.at[slot])

    tab_copy = pltpu.make_async_copy(tab_hbm, tab, tab_sem)
    rec_copy(0).start()
    tab_copy.start()
    rec_copy(1).start()

    barrier = pltpu.get_barrier_semaphore()
    for d in range(1, NTM):
        pl.semaphore_signal(
            barrier, inc=1, device_id=(lax.rem(t + d, NTM), c), device_id_type=MESH
        )
    pl.semaphore_signal(barrier, inc=1, device_id=sibling, device_id_type=MESH)

    @pl.when(jnp.logical_not(first))
    def _():
        pl.semaphore_signal(barrier, inc=1, device_id=before, device_id_type=MESH)

    @pl.when(jnp.logical_not(last))
    def _():
        pl.semaphore_signal(barrier, inc=1, device_id=after, device_id_type=MESH)

    @pl.when(first | last)
    def _():
        for d in range(NTM):
            pl.semaphore_signal(
                barrier, inc=1, device_id=(lax.rem(t + d, NTM), round_corner), device_id_type=MESH
            )

    def clear(i, _):
        acc[i // 16, lax.rem(i, 16)] = jnp.zeros((2, BS, NB), F32)
        return 0

    lax.fori_loop(0, 80, clear, 0)

    rest = jnp.broadcast_to(gain[...].reshape(1, NB), (16, NB))
    total = jnp.zeros((16, EXT), F32)
    for _ in range(3):
        piece = rest.astype(BF16)
        rest = rest - piece.astype(F32)
        total += lax.dot_general(
            piece, perm[...], (((1,), (1,)), ((), ())), preferred_element_type=F32
        )
    gperm[...] = total

    def a2a_copy(w, d):
        q = lax.rem(t + d, NTM)
        return pltpu.make_async_remote_copy(
            src_ref=send.at[w, pl.ds(pl.multiple_of(q * BS, BS), BS)],
            dst_ref=blocks.at[OWN, w, t],
            send_sem=a2a_s.at[w, d],
            recv_sem=a2a_r.at[w, d],
            device_id=(q, c),
            device_id_type=MESH,
        )

    def dup_copy(w, d):
        r = lax.rem(t + d, NTM)
        q = lax.rem(r + shift + NTM, NTM)
        return pltpu.make_async_remote_copy(
            src_ref=send.at[w, pl.ds(pl.multiple_of(q * BS, BS), BS)],
            dst_ref=blocks.at[dup_slot, w, t],
            send_sem=dup_s.at[w, d],
            recv_sem=dup_r.at[w, d],
            device_id=(r, round_corner),
            device_id_type=MESH,
        )

    def bins_of(ref, slot, w, f):
        return ref.at[slot, w, :, :, pl.ds(pl.multiple_of(f * 256, 256), 256)]

    def ring_copy(w, up, f):
        return pltpu.make_async_remote_copy(
            src_ref=bins_of(blocks, OWN, w, f),
            dst_ref=bins_of(blocks, ABOVE if up else BELOW, w, f),
            send_sem=ring_s.at[w, f, up],
            recv_sem=ring_r.at[w, f, up],
            device_id=before if up else after,
            device_id_type=MESH,
        )

    def sib_copy(w, source, slot, f):
        return pltpu.make_async_remote_copy(
            src_ref=bins_of(blocks, source, w, f),
            dst_ref=bins_of(blocks, slot, w, f),
            send_sem=sib_s.at[w, f, slot - X1],
            recv_sem=sib_r.at[w, f, slot - X1],
            device_id=sibling,
            device_id_type=MESH,
        )

    def widen(which, source, w, f):
        at = pl.ds(pl.multiple_of(f * 256, 256), 256)
        to = pl.multiple_of(f * 384, 384)

        def one(i, _):
            both = blocks[source, w, i, :, at].astype(F32)
            wide[which, w, i, :, pl.ds(to, 256)] = both
            wide[which, w, i, :, pl.ds(to + 256, 128)] = both[:, :128] + both[:, 128:]
            return 0

        lax.fori_loop(0, NTM, one, 0, unroll=4)

    def widen_other(slot, to, w, f):
        at = pl.ds(pl.multiple_of(f * 256, 256), 256)

        def one(i, _):
            other[to, i] = blocks[slot, w, i, :, at].astype(F32)
            return 0

        lax.fori_loop(0, NTM, one, 0, unroll=4)

    def spread(w):
        for d in range(1, NTM):
            a2a_copy(w, d).wait_recv()
        for f in range(3):

            @pl.when(jnp.logical_not(first))
            def _():
                ring_copy(w, 1, f).start()

            @pl.when(jnp.logical_not(last))
            def _():
                ring_copy(w, 0, f).start()

            @pl.when(core == 1)
            def _():
                sib_copy(w, OWN, X1, f).start()

        for f in range(3):
            widen(0, OWN, w, f)

    def transform(w, _):
        slot = lax.rem(w, 2)
        rec_copy(w).wait()

        def fold_rows(i, _):
            rows = pl.ds(pl.multiple_of(i * 16, 16), 16)
            low_rows = pl.ds(pl.multiple_of(ROWS + i * 16, 16), 16)

            def put(value, at):
                high = value.astype(BF16)
                fold[rows, at : at + 128] = high
                fold[low_rows, at : at + 128] = (value - high.astype(F32)).astype(BF16)

            for p in range(0, L // 4, 128):
                x0, x1, x2, x3 = (
                    xbuf[slot, rows, s + p : s + p + 128] * hann[:, s + p : s + p + 128]
                    for s in range(0, L, L // 4)
                )
                u, v = x0 + x2, x1 + x3
                put(u + v, p)
                put(u - v, L // 4 + p)
                put(x0 - x2, L // 2 + p)
                put(x1 - x3, 3 * L // 4 + p)
            return 0

        lax.fori_loop(0, ROWS // 16, fold_rows, 0)

        @pl.when(w + 2 < WL)
        def _():
            rec_copy(w + 2).start()

        @pl.when(w == 0)
        def _():
            tab_copy.wait()

        def product(at, length, trow, tcol, col):
            both = jnp.dot(
                fold[:, at : at + length],
                tab[0, trow : trow + length, tcol : tcol + 256],
                preferred_element_type=F32,
            )
            low = jnp.dot(
                fold[:ROWS, at : at + length],
                tab[1, trow : trow + length, tcol : tcol + 256],
                preferred_element_type=F32,
            )
            spec[:, col : col + 256] = both[:ROWS] + (both[ROWS:] + low)

        product(0, L // 4, 0, 0, 0)
        product(L // 4, L // 4, 0, 256, 256)
        product(L // 2, L // 2, L // 4, 0, 512)
        product(L // 2, L // 2, L // 4, 256, 768)

        def spectrum(rows):
            re = jnp.concatenate([spec[rows, 0:128], spec[rows, 256:384], spec[rows, 512:768]], 1)
            im = jnp.concatenate([spec[rows, 128:256], spec[rows, 384:512], spec[rows, 768:1024]], 1)
            return re, im

        def power_rows(i, _):
            rows = pl.ds(pl.multiple_of(i * 16, 16), 16)
            re, im = spectrum(rows)
            power = re * re + im * im
            high = power.astype(BF16)
            pw[rows] = high
            pw[pl.ds(pl.multiple_of(ROWS + i * 16, 16), 16)] = (power - high.astype(F32)).astype(BF16)
            return 0

        lax.fori_loop(0, ROWS // 16, power_rows, 0)
        lev[...] = jnp.dot(pw[...], smooth[...], preferred_element_type=F32)

        def white_rows(i, _):
            rows = pl.ds(pl.multiple_of(i * 16, 16), 16)
            low_rows = pl.ds(pl.multiple_of(ROWS + i * 16, 16), 16)
            level = (lev[rows] + lev[low_rows]) / (2 * HW + 1)
            factor = gperm[...] * lax.rsqrt(level + 1e-6)
            re, im = spectrum(rows)
            wh[rows] = (re * factor).astype(BF16)
            wh[low_rows] = (im * factor).astype(BF16)
            return 0

        lax.fori_loop(0, ROWS // 16, white_rows, 0)
        white = jnp.dot(wh[...], perm[...], preferred_element_type=F32)
        for f in range(3):
            at = f * 256
            send[w, :, at : at + 128] = white[:ROWS, f * 128 : f * 128 + 128].astype(BF16)
            send[w, :, at + 128 : at + 256] = white[ROWS:, f * 128 : f * 128 + 128].astype(BF16)

        @pl.when((w == 0) & jnp.logical_not(first | last))
        def _():
            pl.semaphore_wait(barrier, NTM - 1 + 3)

        @pl.when((w == 0) & (first | last))
        def _():
            pl.semaphore_wait(barrier, NTM - 1 + 2 + NTM)

        for d in range(1, NTM):
            a2a_copy(w, d).start()
        blocks[OWN, w, t] = send[w, pl.ds(pl.multiple_of(t * BS, BS), BS)]

        @pl.when((w > 0) & (first | last))
        def _():
            for d in range(NTM):
                dup_copy(w - 1, d).start()

        @pl.when(w > 0)
        def _():
            spread(w - 1)

        return 0

    lax.fori_loop(0, WL, transform, 0)

    @pl.when(first | last)
    def _():
        for d in range(NTM):
            dup_copy(WL - 1, d).start()

    def correlate(k, left, right, w, f):
        re_at = pl.ds(pl.multiple_of(f * 384, 128), 128)
        im_at = pl.ds(pl.multiple_of(f * 384 + 128, 128), 128)
        sum_at = pl.ds(pl.multiple_of(f * 384 + 256, 128), 128)
        at = pl.ds(pl.multiple_of(f * 128, 128), 128)
        zero = jnp.zeros((BS, 128), F32)
        for part in range(4):
            mine = range(part * 4, part * 4 + 4)

            def window(n, sums):
                if right is None:
                    cr = wide[0, w, n, :, re_at]
                    ci = wide[0, w, n, :, im_at]
                else:
                    cr = other[right, n, :, :128]
                    ci = other[right, n, :, 128:]
                plus, minus = cr + ci, cr - ci
                new = []
                for i, a in enumerate(mine):
                    new.append(sums[3 * i] + wide[left, w, n, a : a + 1, sum_at] * cr)
                    new.append(sums[3 * i + 1] + wide[left, w, n, a : a + 1, re_at] * plus)
                    new.append(sums[3 * i + 2] + wide[left, w, n, a : a + 1, im_at] * minus)
                return tuple(new)

            sums = lax.fori_loop(0, NTM, window, (zero,) * 12, unroll=8)
            for i, a in enumerate(mine):
                acc[k, a, 0, :, at] += sums[3 * i] - sums[3 * i + 2]
                acc[k, a, 1, :, at] += sums[3 * i] - sums[3 * i + 1]

    def selfs(i, _):
        correlate(0, 0, None, i // 3, lax.rem(i, 3))
        return 0

    lax.fori_loop(0, 3 * (WL - 1), selfs, 0)
    spread(WL - 1)
    lax.fori_loop(3 * (WL - 1), 3 * WL, selfs, 0)

    def give_copy(i, f):
        return pltpu.make_async_remote_copy(
            src_ref=give.at[i, f],
            dst_ref=take.at[i, f],
            send_sem=give_s.at[i, f],
            recv_sem=give_r.at[i, f],
            device_id=before,
            device_id_type=MESH,
        )

    def hand_over(i, k, f):
        at = pl.ds(pl.multiple_of(f * 128, 128), 128)

        def one(a, _):
            give[i, f, a] = acc[k, a, :, :, at].astype(BF16)
            return 0

        lax.fori_loop(0, BS, one, 0, unroll=4)
        give_copy(i, f).start()

    left3 = core
    right3 = X2 - core - ABOVE

    def arrive(i):
        w = i // 3
        f = lax.rem(i, 3)

        @pl.when(jnp.logical_not(last))
        def _():
            ring_copy(w, 1, f).wait_recv()

        @pl.when(jnp.logical_not(first))
        def _():
            ring_copy(w, 0, f).wait_recv()

        @pl.when((first | last) & (f == 0))
        def _():
            for d in range(NTM):
                dup_copy(w, d).wait_recv()

        @pl.when(core == 0)
        def _():
            sib_copy(w, ABOVE, X1, f).start()

        @pl.when(core == 1)
        def _():
            sib_copy(w, ABOVE, X2, f).start()

        widen(1, BELOW, w, f)
        above = 3 * lax.rem(i, 2)
        widen_other(ABOVE, above, w, f)
        correlate(4, 1, above, w, f)

        @pl.when(w == WL - 1)
        def _():
            hand_over(0, 4, f)


    def use_shared(i):
        w = i // 3
        f = lax.rem(i, 3)
        sib_copy(w, OWN, X1, f).wait_recv()
        widen_other(X1, 1, w, f)

        @pl.when(core == 0)
        def _():
            sib_copy(w, OWN, X2, f).wait_recv()
            widen_other(X2, 2, w, f)

        correlate(3, left3, right3, w, f)

        @pl.when((w == WL - 1) & (core == 1))
        def _():
            hand_over(1, 3, f)

        correlate(1, 0, 1, w, f)
        correlate(2, 0, 3 * lax.rem(i, 2), w, f)

    def partners(i, _):
        @pl.when(i < 3 * WL)
        def _():
            arrive(i)

        @pl.when(i > 0)
        def _():
            use_shared(i - 1)

        return 0

    def out_copy(k, p):
        return pltpu.make_async_copy(acc.at[k, :, p], out.at[k, :, p], out_sem.at[k, p])

    def weight_of(k):
        inside = (block + k < NBLK).astype(F32)
        return mask[0, k].astype(F32) * inside * (1.0 / 64.0)

    def finish(k):
        weight = weight_of(k)

        def one(a, _):
            acc[k, a] = acc[k, a] * weight
            return 0

        lax.fori_loop(0, BS, one, 0, unroll=2)
        for p in range(2):
            out_copy(k, p).start()

    def finish_taken(k, i):
        weight = weight_of(k)
        for f in range(3):
            give_copy(i, f).wait_recv()

            def one(a, _):
                acc[k, a, :, :, f * 128 : f * 128 + 128] = take[i, f, a].astype(F32) * weight
                return 0

            lax.fori_loop(0, BS, one, 0, unroll=4)
        for p in range(2):
            out_copy(k, p).start()

    finish(0)
    lax.fori_loop(0, 3 * WL + 1, partners, 0)

    finish(2)
    finish(1)

    @pl.when(core == 0)
    def _():
        finish(3)

    finish_taken(4, 0)

    @pl.when(core == 1)
    def _():
        finish_taken(3, 1)

    def drain(i, _):
        w = i // 3
        f = lax.rem(i, 3)

        @pl.when(f == 0)
        def _():
            for d in range(1, NTM):
                a2a_copy(w, d).wait_send()

        @pl.when((first | last) & (f == 0))
        def _():
            for d in range(NTM):
                dup_copy(w, d).wait_send()

        @pl.when(jnp.logical_not(first))
        def _():
            ring_copy(w, 1, f).wait_send()

        @pl.when(jnp.logical_not(last))
        def _():
            ring_copy(w, 0, f).wait_send()

        @pl.when(core == 0)
        def _():
            sib_copy(w, ABOVE, X1, f).wait_send()

        @pl.when(core == 1)
        def _():
            sib_copy(w, OWN, X1, f).wait_send()
            sib_copy(w, ABOVE, X2, f).wait_send()

        return 0

    lax.fori_loop(0, 3 * WL, drain, 0)
    for f in range(3):
        give_copy(0, f).wait_send()

        @pl.when(core == 1)
        def _():
            give_copy(1, f).wait_send()

    for k in range(5):
        for p in range(2):
            out_copy(k, p).wait()


def place_kernel(sums, out, held, in_sem, out_sem):
    def take_in(k):
        return pltpu.make_async_copy(sums.at[k], held.at[k], in_sem.at[k])

    def put_out(k, p):
        return pltpu.make_async_copy(held.at[k, :, p], out.at[k, :, :, p], out_sem.at[k, p])

    for k in range(5):
        take_in(k).start()
    for k in range(5):
        take_in(k).wait()
        for p in range(2):
            put_out(k, p).start()
    for k in range(5):
        for p in range(2):
            put_out(k, p).wait()


def body(records, band_gain, pair_mask):
    rec = records.reshape(WL, ROWS, L)
    any_space = pl.BlockSpec(memory_space=pl.ANY)
    vmem = pl.BlockSpec(memory_space=pltpu.VMEM)
    smem = pl.BlockSpec(memory_space=pltpu.SMEM)
    dma = pltpu.SemaphoreType.DMA
    sums = pl.pallas_call(
        kernel,
        out_shape=jax.ShapeDtypeStruct((5, BS, 2, BS, NB), F32),
        in_specs=[any_space, any_space, vmem, vmem, vmem, vmem, smem],
        out_specs=any_space,
        scratch_shapes=[
            pltpu.VMEM((2, ROWS, L), F32),
            pltpu.VMEM((2, 3 * L // 4, 512), BF16),
            pltpu.VMEM((2 * ROWS, L), BF16),
            pltpu.VMEM((ROWS, 2 * EXT), F32),
            pltpu.VMEM((2 * ROWS, EXT), BF16),
            pltpu.VMEM((2 * ROWS, EXT), F32),
            pltpu.VMEM((2 * ROWS, EXT), BF16),
            pltpu.VMEM((16, EXT), F32),
            pltpu.VMEM((WL, ROWS, 2 * NB), BF16),
            pltpu.VMEM((5, WL, NTM, BS, 2 * NB), BF16),
            pltpu.VMEM((2, WL, NTM, BS, 3 * NB), F32),
            pltpu.VMEM((4, NTM, BS, 256), F32),
            pltpu.VMEM((5, BS, 2, BS, NB), F32),
            pltpu.VMEM((2, 3, BS, 2, BS, 128), BF16),
            pltpu.VMEM((2, 3, BS, 2, BS, 128), BF16),
            dma((2,)),
            dma,
            dma((WL, NTM)),
            dma((WL, NTM)),
            dma((WL, NTM)),
            dma((WL, NTM)),
            dma((WL, 3, 2)),
            dma((WL, 3, 2)),
            dma((WL, 3, 2)),
            dma((WL, 3, 2)),
            dma((2, 3)),
            dma((2, 3)),
            dma((5, 2)),
        ],
        compiler_params=pltpu.CompilerParams(
            collective_id=0, has_side_effects=True, vmem_limit_bytes=58 << 20
        ),
        cost_estimate=pl.CostEstimate(
            flops=10**10, bytes_accessed=30 * 10**6, transcendentals=10**6
        ),
    )(
        rec,
        jnp.asarray(dft_tables()),
        jnp.asarray(smoother_table()),
        jnp.asarray(order_table()),
        jnp.asarray(hann_row()),
        band_gain,
        pair_mask,
    )
    stacks = pl.pallas_call(
        place_kernel,
        out_shape=jax.ShapeDtypeStruct((5, BS, BS, 2, NB), F32),
        in_specs=[any_space],
        out_specs=any_space,
        scratch_shapes=[pltpu.VMEM((5, BS, 2, BS, NB), F32), dma((5,)), dma((5, 2))],
        cost_estimate=pl.CostEstimate(flops=0, bytes_accessed=8 * 10**6, transcendentals=0),
    )(sums)
    return stacks[None]


def solution(mesh):
    placed = (P("tm", None, "chan", None, None), P(), P(("tm", "chan"), None))
    return jax.shard_map(
        body,
        mesh=mesh,
        in_specs=placed,
        out_specs=P(("tm", "chan"), None, None, None, None, None),
        check_vma=False,
    )
```
